256 devices in a mesh: slab: 2 (over core), scan: 128 (over y, x, z).
Axes of the slice: x: 4, y: 4, z: 8, core: 2. Of those that a mesh axis runs over, the one named last changes fastest.
Arguments:
- probe_modes: bfloat16 [4, 256, 512], replicated, may hold values from -6 to 6
- tap_weights: bfloat16 [2, 2, 31], replicated, may hold values from -0.75 to 0.75
- object_slices: float32 [2, 1024, 128, 256], P('slab', 'scan'), may hold values from -5 to 5
- exit_residual: bfloat16 [128, 2, 4, 256, 512], P('scan'), may hold values from -6 to 6
- offsets: int32 [128, 2, 2], P('scan'), may hold values from 0 to 127
- owners: int32 [128, 2, 9], P('scan'), may hold values from 0 to 1023, as said below
Outputs:
- updated_slices: float32 [2, 1024, 128, 256], P('slab', 'scan')
The draws below stay inside these ranges and needn't reach their ends.
Inputs may be any that keep to these rules, and one draw needn't show every extreme that they name: `owners`: for position p of group g, entry 3 i + j names the tile in block row i and block column j; its value is c * 8 + q, with c = (g - 1 + j) mod 128 the group that holds the tile and q one of its 8 slots. The nine entries of a position are distinct.
All inputs are finite; a program needn't handle non-finite values.
Results may differ from the reference program's by a relative error of at most 0.01.
Values may be sent and summed in bfloat16 or wider, within the bound.
No kernel may reach another device: no remote copies, remote signals or barrier semaphores. Data moves between devices by JAX's collectives and lax.ppermute only.
A program may use at most 64 MiB of HBM per device.

```python
import jax
import jax.numpy as jnp
from jax import lax

NP = 256
TS = 128
TAPS = 31
MODES = 4
POS = 2
CAP = 8
SLICES = 2
GROUPS = 128
TILES = 1024


def draw_owners(key, part):
    key_order = jax.random.fold_in(key, 11)
    key_rows = jax.random.fold_in(key, 23)
    scores = jax.random.randint(key_order, (GROUPS, CAP), 0, 1 << 20) * CAP + jnp.arange(CAP)[None, :]
    slot_order = jnp.argsort(scores, axis=1).astype(jnp.int32)
    first_rows = jax.random.randint(key_rows, (GROUPS, POS), 0, CAP - 2)
    first_rows = first_rows.at[0, 0].set(0).at[0, POS - 1].set(CAP - 3)
    columns = (jnp.arange(GROUPS)[:, None] - 1 + jnp.arange(3)[None, :]) % GROUPS
    rows_used = first_rows[:, :, None] + jnp.arange(3)[None, None, :]
    column_grid = jnp.broadcast_to(columns[:, None, None, :], (GROUPS, POS, 3, 3))
    row_grid = jnp.broadcast_to(rows_used[:, :, :, None], (GROUPS, POS, 3, 3))
    slot_grid = slot_order[column_grid, row_grid]
    return (column_grid * CAP + slot_grid).reshape(GROUPS, POS, 9).astype(jnp.int32)


def plant(values, rng, least, top_value):
    index_at = [jax.random.randint(jax.random.fold_in(rng, axis), (), 0, length) for axis, length in enumerate(values.shape)]
    widest = values.shape.index(max(values.shape))
    neighbour = index_at[:widest] + [(index_at[widest] + 1) % values.shape[widest]] + index_at[widest + 1:]
    return values.at[tuple(index_at)].set(least).at[tuple(neighbour)].set(top_value)


def shard_levels(key, shape, cuts, least, top_value):
    gain, own = 1.0, jax.random.fold_in(key, 6)
    for dim, parts in cuts:
        draws = jnp.exp(jax.random.uniform(jax.random.fold_in(own, dim), (parts,), jnp.float32, least / len(cuts), top_value / len(cuts)))
        gain = gain * jnp.repeat(draws, shape[dim] // parts).reshape([-1 if axis == dim else 1 for axis in range(len(shape))])
    return gain


def bell_draw(own_key, dims, width, bound, split=(), kind=jnp.bfloat16):
    level = shard_levels(own_key, dims, split, -0.22, 0.18) if split else 1.0
    entries = jax.random.normal(own_key, dims, jnp.float32) * width * level
    return jnp.minimum(jnp.maximum(entries, -bound), bound).astype(kind)


def setup_inputs(seed: int = 0) -> dict:
    arg_keys = jax.random.split(jax.random.key(seed), 7)
    return {
        "probe_modes": bell_draw(arg_keys[0], (MODES, NP, 2 * NP), 1.0, 6.0),
        "tap_weights": bell_draw(arg_keys[1], (2, 2, TAPS), (2 * TAPS) ** -0.5, 0.75),
        "object_slices": bell_draw(arg_keys[2], (SLICES, TILES, TS, 2 * TS), 0.7071, 5.0, ((0, 2), (1, 128)), jnp.float32),
        "exit_residual": bell_draw(arg_keys[3], (GROUPS, POS, MODES, NP, 2 * NP), 1.0, 6.0, ((0, 128),)),
        "offsets": plant(jax.random.randint(arg_keys[4], (GROUPS, POS, 2), 0, TS), jax.random.fold_in(arg_keys[4], 1), 0, TS - 1).astype(jnp.int32),
        "owners": draw_owners(jax.random.fold_in(arg_keys[6], 71), 0),
    }


step_rate = 0.125


def band_matrix(weights, extent):
    tap_count = weights.shape[0]
    half_width = (tap_count - 1) // 2
    tap_line = jnp.concatenate([weights[half_width:], jnp.zeros((2 * extent - 1 - tap_count,), weights.dtype), weights[:half_width]])
    repeated = jnp.tile(tap_line, extent)
    return repeated[: extent * (2 * extent - 2)].reshape(extent, 2 * extent - 2)[:, :extent]


def kernels(tap_weights, extent):
    rows_re = band_matrix(tap_weights[0, 0], extent)
    rows_im = band_matrix(tap_weights[0, 1], extent)
    cols_re = band_matrix(tap_weights[1, 0], extent)
    cols_im = band_matrix(tap_weights[1, 1], extent)
    left_mat = jnp.concatenate([rows_re, rows_im], 0)
    left_adj = jnp.concatenate([rows_re.T, rows_im.T], 0)
    right_mat = jnp.concatenate([jnp.concatenate([cols_re.T, cols_im.T], 1), jnp.concatenate([-cols_im.T, cols_re.T], 1)], 0)
    return left_mat, left_adj, right_mat


def matmul(spec, left_op, right_op):
    return jnp.einsum(spec, left_op.astype(jnp.float32), right_op.astype(jnp.float32), precision=lax.Precision.HIGHEST)


def combine(product, extent, sign_flip):
    top_half = product[..., :extent, :]
    low_half = product[..., extent:, :]
    real_part = top_half[..., :extent] - sign_flip * low_half[..., extent:]
    imag_part = top_half[..., extent:] + sign_flip * low_half[..., :extent]
    return jnp.concatenate([real_part, imag_part], -1)


def propagate(wavefield, matrices):
    extent = wavefield.shape[-2]
    mixed_rows = combine(matmul("rk,...kc->...rc", matrices[0], wavefield), extent, 1.0).astype(jnp.bfloat16)
    return matmul("...rk,kc->...rc", mixed_rows, matrices[2]).astype(jnp.bfloat16)


def adjoint(wavefield, matrices):
    extent = wavefield.shape[-2]
    mixed_rows = matmul("...rk,ck->...rc", wavefield, matrices[2]).astype(jnp.bfloat16)
    return combine(matmul("rk,...kc->...rc", matrices[1], mixed_rows), extent, -1.0).astype(jnp.bfloat16)


def complex_product(left_op, right_op, conjugate):
    extent = left_op.shape[-1] // 2
    left_re = left_op[..., :extent].astype(jnp.float32)
    left_im = left_op[..., extent:].astype(jnp.float32)
    right_re = right_op[..., :extent].astype(jnp.float32)
    right_im = right_op[..., extent:].astype(jnp.float32)
    if conjugate:
        real_part = left_re * right_re + left_im * right_im
        imag_part = left_re * right_im - left_im * right_re
    else:
        real_part = left_re * right_re - left_im * right_im
        imag_part = left_re * right_im + left_im * right_re
    return jnp.concatenate([real_part, imag_part], -1)


def assemble(tiles, row_shift, col_shift, extent):
    layers = tiles.shape[0]
    tile_side = tiles.shape[-2]
    tile_grid = tiles.reshape(layers, 3, 3, tile_side, 2, tile_side)
    corner = (jnp.zeros((), jnp.int32), row_shift.astype(jnp.int32), col_shift.astype(jnp.int32))
    halves = []
    for part_index in range(2):
        full_block = tile_grid[:, :, :, :, part_index, :].transpose(0, 1, 3, 2, 4).reshape(layers, 3 * tile_side, 3 * tile_side)
        halves.append(lax.dynamic_slice(full_block, corner, (layers, extent, extent)))
    return jnp.concatenate(halves, -1)


def disassemble(window_terms, row_shift, col_shift, tile_side):
    layers = window_terms.shape[0]
    extent = window_terms.shape[-2]
    corner = (jnp.zeros((), jnp.int32), row_shift.astype(jnp.int32), col_shift.astype(jnp.int32))
    halves = []
    for part_index in range(2):
        empty_block = jnp.zeros((layers, 3 * tile_side, 3 * tile_side), window_terms.dtype)
        placed = lax.dynamic_update_slice(empty_block, window_terms[..., part_index * extent:(part_index + 1) * extent], corner)
        halves.append(placed.reshape(layers, 3, tile_side, 3, tile_side).transpose(0, 1, 3, 2, 4).reshape(layers, 9, tile_side, tile_side))
    return jnp.concatenate(halves, -1)


def forward(wavefield, windows, matrices, finish):
    inputs = []
    layer_count = windows.shape[0]
    for layer_index in range(layer_count):
        inputs.append(wavefield)
        if layer_index + 1 < layer_count or finish:
            product = complex_product(wavefield, windows[layer_index][:, None], False).astype(jnp.bfloat16)
            wavefield = propagate(product, matrices)
    return jnp.stack(inputs), wavefield


def backward(incoming, inputs, windows, matrices, finish):
    layer_count = windows.shape[0]
    slice_terms = [None] * layer_count
    for layer_index in reversed(range(layer_count)):
        adjoint_wave = adjoint(incoming, matrices)
        slice_terms[layer_index] = jnp.sum(complex_product(inputs[layer_index], adjoint_wave, True), axis=1)
        if layer_index > 0 or finish:
            incoming = complex_product(windows[layer_index][:, None], adjoint_wave, True).astype(jnp.bfloat16)
    return jnp.stack(slice_terms), incoming


def reference(probe_modes, tap_weights, object_slices, exit_residual, offsets, owners):
    extent = probe_modes.shape[-2]
    tile_side = object_slices.shape[-2]
    positions = offsets.shape[1]
    matrices = kernels(tap_weights, extent)
    rounded = object_slices.astype(jnp.bfloat16)
    starts = jnp.broadcast_to(probe_modes[None], (positions,) + probe_modes.shape)

    def one_group(gradient_sum, group_items):
        residual_group, offset_group, owner_group = group_items
        window_list = []
        for item_index in range(positions):
            tiles = jnp.take(rounded, owner_group[item_index], axis=1)
            window_list.append(assemble(tiles, offset_group[item_index, 0], offset_group[item_index, 1], extent))
        windows = jnp.stack(window_list, 1)
        inputs = forward(starts, windows, matrices, False)[0]
        window_terms = backward(residual_group, inputs, windows, matrices, False)[0]
        pieces = []
        for item_index in range(positions):
            pieces.append(disassemble(window_terms[:, item_index], offset_group[item_index, 0], offset_group[item_index, 1], tile_side))
        stacked = jnp.concatenate(pieces, 1)
        gradient_sum = gradient_sum.at[:, owner_group.reshape(-1)].add(stacked)
        return gradient_sum, None

    gradient_sum, unused = lax.scan(one_group, jnp.zeros(object_slices.shape, jnp.float32), (exit_residual, offsets, owners))
    return object_slices - step_rate * gradient_sum
```

```python
import functools

import jax
import jax.numpy as jnp
from jax import lax
from jax.experimental import pallas as pl
from jax.experimental.pallas import tpu as pltpu
from jax.sharding import PartitionSpec as P

step_rate = 0.125
F32, BF16 = jnp.float32, jnp.bfloat16
NP, TS, HALF = 256, 128, 15
MODES, POS, CAP = 4, 2, 8
ROWS = CAP * TS
SMEM = pl.BlockSpec(memory_space=pltpu.SMEM)
VMEM = pl.BlockSpec(memory_space=pltpu.VMEM)


def params(mib):
    return pltpu.CompilerParams(vmem_limit_bytes=mib * 1024 * 1024)


def dot(left, right):
    return jnp.dot(left, right, preferred_element_type=F32)


def lanes(rows):
    return lax.broadcasted_iota(jnp.int32, (rows, TS), 1)


def pack_kernel(owners, offsets, tiles, out):
    for q in range(CAP):
        out[q * TS : (q + 1) * TS, :] = tiles[0, q].astype(BF16)
    spot = lax.broadcasted_iota(jnp.int32, (16, 2 * TS), 1)
    notes = jnp.zeros((16, 2 * TS), jnp.int32)
    for p in range(POS):
        for k in range(9):
            notes = jnp.where(spot == p * 16 + k, owners[0, p, k] & (CAP - 1), notes)
        notes = jnp.where(spot == p * 16 + 9, offsets[0, p, 0], notes)
    out[ROWS : ROWS + 16, :] = notes.astype(F32).astype(BF16)


def pack(owners, offsets, tiles):
    return pl.pallas_call(
        pack_kernel,
        out_shape=jax.ShapeDtypeStruct((ROWS + 16, 2 * TS), BF16),
        in_specs=[SMEM, SMEM, VMEM],
        out_specs=VMEM,
        compiler_params=params(8),
        name="pack_tiles",
    )(owners, offsets, tiles)


def band(taps, row):
    wide = jnp.broadcast_to(taps[row : row + 1, :], (NP, NP))
    turned = pltpu.roll(wide, NP - HALF, 1, stride=1, stride_axis=0)
    gap = lax.broadcasted_iota(jnp.int32, (NP, NP), 1) - lax.broadcasted_iota(jnp.int32, (NP, NP), 0)
    return jnp.where(jnp.abs(gap) <= HALF, turned, 0.0)


def exit_kernel(taps, residual, left, left_adj, right, right_adj, wave, line):
    line[...] = jnp.zeros_like(line)
    for row in range(4):
        line[row : row + 1, 0 : 2 * HALF + 1] = taps[row // 2, row % 2 : row % 2 + 1, :].astype(F32)
    values = line[...]
    for first, plain, adj in ((0, left, left_adj), (2, right_adj, right)):
        re, im = band(values, first), band(values, first + 1)
        ret, imt = re.T, im.T
        plain[0:NP, 0:NP] = re.astype(BF16)
        plain[0:NP, NP:] = (-im).astype(BF16)
        plain[NP:, 0:NP] = im.astype(BF16)
        plain[NP:, NP:] = re.astype(BF16)
        adj[0:NP, 0:NP] = ret.astype(BF16)
        adj[0:NP, NP:] = imt.astype(BF16)
        adj[NP:, 0:NP] = (-imt).astype(BF16)
        adj[NP:, NP:] = ret.astype(BF16)
    for m in range(MODES):
        w = dot(residual[0, 0, m], right_adj[...]).astype(BF16)
        w = jnp.concatenate([w[:, :NP], w[:, NP:]], 0)
        wave[m] = dot(left_adj[...], w).astype(BF16)


def exit_adjoint(side, taps, residual):
    whole = lambda *shape: pl.BlockSpec(shape, lambda i, side: (0,) * len(shape))
    return pl.pallas_call(
        lambda side, *refs: exit_kernel(*refs),
        grid_spec=pltpu.PrefetchScalarGridSpec(
            num_scalar_prefetch=1,
            grid=(1,),
            in_specs=[
                whole(2, 2, 2 * HALF + 1),
                pl.BlockSpec((1, 1, MODES, NP, 2 * NP), lambda i, side: (0, side[0], 0, 0, 0)),
            ],
            out_specs=[whole(2 * NP, 2 * NP)] * 4 + [whole(MODES, 2 * NP, NP)],
            scratch_shapes=[pltpu.VMEM((8, NP), F32)],
        ),
        out_shape=[jax.ShapeDtypeStruct((2 * NP, 2 * NP), BF16)] * 4
        + [jax.ShapeDtypeStruct((MODES, 2 * NP, NP), BF16)],
        compiler_params=params(24),
        cost_estimate=pl.CostEstimate(flops=1_100_000_000, bytes_accessed=6_000_000, transcendentals=0),
        name="exit_adjoint",
    )(side, taps, residual)


def cut_window(p, owners, offsets, sources, stack, out):
    r, c = offsets[0, p, 0], offsets[0, p, 1]
    for j, tiles in enumerate(sources):
        for i in range(3):
            q = owners[0, p, 3 * i + j] & (CAP - 1)
            tile = tiles[pl.ds(pl.multiple_of(q * TS, TS), TS), :].astype(F32)
            stack[j, 0, i * TS : (i + 1) * TS, :] = tile[:, :TS]
            stack[j, 1, i * TS : (i + 1) * TS, :] = tile[:, TS:]
    back = (TS - c) & (TS - 1)
    step = 32
    near = lanes(step) < TS - c
    for at in range(0, NP, step):
        for part in range(2):
            cols = [pltpu.roll(stack[j, part, pl.ds(r + at, step), :], back, 1) for j in range(3)]
            out[part, at : at + step, 0:TS] = jnp.where(near, cols[0], cols[1]).astype(out.dtype)
            out[part, at : at + step, TS:] = jnp.where(near, cols[1], cols[2]).astype(out.dtype)


def window_kernel(owners, offsets, before, own, after, out, stack):
    p = 1 - lax.axis_index("slab")
    cut_window(p, owners, offsets, (before, own, after), stack, out)


def far_window(owners, offsets, before, own, after):
    return pl.pallas_call(
        window_kernel,
        out_shape=jax.ShapeDtypeStruct((2, NP, NP), BF16),
        in_specs=[SMEM, SMEM, VMEM, VMEM, VMEM],
        out_specs=VMEM,
        scratch_shapes=[pltpu.VMEM((3, 2, 3 * TS, TS), F32)],
        compiler_params=params(8),
        cost_estimate=pl.CostEstimate(flops=1_000_000, bytes_accessed=2_000_000, transcendentals=0),
        name="far_window",
    )(owners, offsets, before, own, after)


def times(a, b, conjugate):
    (ar, ai), (br, bi) = a, b
    if conjugate:
        return ar * br + ai * bi, ar * bi - ai * br
    return ar * br - ai * bi, ar * bi + ai * br


def beside(ref, m):
    return ref[m, :, :NP].astype(F32), ref[m, :, NP:].astype(F32)


def above(ref, m):
    return ref[m, :NP, :].astype(F32), ref[m, NP:, :].astype(F32)


def lower_terms(t, probe, wave, left, right, total):
    for m in range(MODES):
        window = (t[0].astype(F32), t[1].astype(F32))
        u = jnp.concatenate(times(beside(probe, m), window, False), 0).astype(BF16)
        v = dot(left[...], u).astype(BF16)
        v = jnp.concatenate([v[:NP], v[NP:]], 1)
        psi = dot(v, right[...]).astype(BF16).astype(F32)
        re, im = times((psi[:, :NP], psi[:, NP:]), above(wave, m), True)
        if m == 0:
            total[0], total[1] = re, im
        else:
            total[0] += re
            total[1] += im


def upper_terms(t, probe, wave, left_adj, right_adj, total):
    for m in range(MODES):
        window = (t[0].astype(F32), t[1].astype(F32))
        b = jnp.concatenate(times(window, above(wave, m), True), 1).astype(BF16)
        w = dot(b, right_adj[...]).astype(BF16)
        w = jnp.concatenate([w[:, :NP], w[:, NP:]], 0)
        a = dot(left_adj[...], w).astype(BF16).astype(F32)
        re, im = times(beside(probe, m), (a[:NP], a[NP:]), True)
        if m == 0:
            total[0], total[1] = re, im
        else:
            total[0] += re
            total[1] += im


def both_ways(chosen, t, probe, wave, left, left_adj, right, right_adj, total):
    @pl.when(chosen == 0)
    def _():
        lower_terms(t, probe, wave, left, right, total)

    @pl.when(chosen == 1)
    def _():
        upper_terms(t, probe, wave, left_adj, right_adj, total)


def near_kernel(owners, offsets, before, own, after, probe, wave, left, left_adj, right, right_adj, out, stack, t, total):
    side = lax.axis_index("slab")
    cut_window(side, owners, offsets, (before, own, after), stack, t)
    both_ways(side, t, probe, wave, left, left_adj, right, right_adj, total)
    out[...] = total[...].astype(BF16)


def far_kernel(t, probe, wave, left, left_adj, right, right_adj, out):
    side = lax.axis_index("slab")
    both_ways(1 - side, t, probe, wave, left, left_adj, right, right_adj, out)


COST = pl.CostEstimate(flops=1_100_000_000, bytes_accessed=5_000_000, transcendentals=0)


def near_terms(owners, offsets, before, own, after, probe, wave, mats):
    return pl.pallas_call(
        near_kernel,
        out_shape=jax.ShapeDtypeStruct((2, NP, NP), BF16),
        in_specs=[SMEM, SMEM] + [VMEM] * 9,
        out_specs=VMEM,
        scratch_shapes=[
            pltpu.VMEM((3, 2, 3 * TS, TS), F32),
            pltpu.VMEM((2, NP, NP), F32),
            pltpu.VMEM((2, NP, NP), F32),
        ],
        compiler_params=params(24),
        cost_estimate=COST,
        name="near_terms",
    )(owners, offsets, before, own, after, probe, wave, *mats)


def far_terms(t, probe, wave, mats):
    return pl.pallas_call(
        far_kernel,
        out_shape=jax.ShapeDtypeStruct((2, NP, NP), F32),
        in_specs=[VMEM] * 7,
        out_specs=VMEM,
        compiler_params=params(24),
        cost_estimate=COST,
        name="far_terms",
    )(t, probe, wave, *mats)


def split_kernel(offsets, mine, others, before, own, after):
    side = lax.axis_index("slab")
    step = 32
    spot = lanes(step)
    for k, terms in ((0, mine), (1, others)):
        p = side if k == 0 else 1 - side
        c = offsets[0, p, 1]
        for at in range(0, NP, step):
            for part in range(2):
                low = pltpu.roll(terms[part, at : at + step, 0:TS].astype(F32), c, 1)
                high = pltpu.roll(terms[part, at : at + step, TS:].astype(F32), c, 1)
                place = (pl.ds(p * NP + at, step), slice(part * TS, (part + 1) * TS))
                before[place] = jnp.where(spot >= c, low, 0.0).astype(BF16)
                own[place] = jnp.where(spot < c, low, high)
                after[place] = jnp.where(spot < c, high, 0.0).astype(BF16)


def split_terms(offsets, mine, others):
    shape = (POS * NP, 2 * TS)
    return pl.pallas_call(
        split_kernel,
        out_shape=[
            jax.ShapeDtypeStruct(shape, BF16),
            jax.ShapeDtypeStruct(shape, F32),
            jax.ShapeDtypeStruct(shape, BF16),
        ],
        in_specs=[SMEM, VMEM, VMEM],
        out_specs=[VMEM] * 3,
        compiler_params=params(8),
        name="split_terms",
    )(offsets, mine, others)


def take_off(terms, slot, row, stack, out):
    for p in range(POS):
        for part in range(2):
            cols = slice(part * TS, (part + 1) * TS)
            stack[part, TS : TS + NP, :] = terms[p * NP : (p + 1) * NP, cols].astype(F32) * step_rate
        r = row(p)
        for i in range(3):
            for part in range(2):
                cols = slice(part * TS, (part + 1) * TS)
                out[0, slot(p, i), :, cols] -= stack[part, pl.ds(TS + i * TS - r, TS), :]


def clear(stack):
    stack[:, 0:TS, :] = jnp.zeros((2, TS, TS), F32)
    stack[:, TS + NP :, :] = jnp.zeros((2, TS, TS), F32)


def own_kernel(owners, offsets, tiles, terms, out, stack):
    clear(stack)
    out[...] = tiles[...]
    take_off(terms, lambda p, i: owners[0, p, 3 * i + 1] & (CAP - 1), lambda p: offsets[0, p, 0], stack, out)


def own_update(owners, offsets, tiles, terms):
    return pl.pallas_call(
        own_kernel,
        out_shape=jax.ShapeDtypeStruct(tiles.shape, F32),
        in_specs=[SMEM, SMEM, VMEM, VMEM],
        out_specs=VMEM,
        scratch_shapes=[pltpu.VMEM((2, 2 * TS + NP, TS), F32)],
        compiler_params=params(8),
        cost_estimate=pl.CostEstimate(flops=1_000_000, bytes_accessed=3_000_000, transcendentals=0),
        name="own_update",
    )(owners, offsets, tiles, terms)


def last_kernel(notes_left, notes_right, tiles, from_left, from_right, out, stack):
    clear(stack)
    out[...] = tiles[...]
    take_off(from_right, lambda p, i: notes_right[0, p * 16 + 3 * i], lambda p: notes_right[0, p * 16 + 9], stack, out)
    take_off(from_left, lambda p, i: notes_left[0, p * 16 + 3 * i + 2], lambda p: notes_left[0, p * 16 + 9], stack, out)


def last_update(notes_left, notes_right, tiles, from_left, from_right):
    return pl.pallas_call(
        last_kernel,
        out_shape=jax.ShapeDtypeStruct(tiles.shape, F32),
        in_specs=[SMEM, SMEM, VMEM, VMEM, VMEM],
        out_specs=VMEM,
        scratch_shapes=[pltpu.VMEM((2, 2 * TS + NP, TS), F32)],
        compiler_params=params(8),
        name="last_update",
    )(notes_left, notes_right, tiles, from_left, from_right)


def along(value, distance):
    count = lax.axis_size("scan")
    return lax.ppermute(value, "scan", [(i, (i + distance) % count) for i in range(count)])


def across(value):
    return lax.ppermute(value, "slab", [(0, 1), (1, 0)])


def shards(probe_modes, tap_weights, object_slices, exit_residual, offsets, owners):
    side = lax.axis_index("slab").astype(jnp.int32).reshape(1)
    own = pack(owners, offsets, object_slices)
    before, after = along(own, 1), along(own, -1)
    *mats, wave = exit_adjoint(side, tap_weights, exit_residual)
    t_there = far_window(owners, offsets, before, own, after)
    t_here = across(t_there)
    terms_there = near_terms(owners, offsets, before, own, after, probe_modes, wave, mats)
    terms_far = across(terms_there)
    terms_here = far_terms(t_here, probe_modes, wave, mats)
    to_left, kept, to_right = split_terms(offsets, terms_here, terms_far)
    from_right, from_left = along(to_left, -1), along(to_right, 1)
    partly = own_update(owners, offsets, object_slices, kept)
    notes_left = before[ROWS : ROWS + 1, : 2 * 16].astype(jnp.int32)
    notes_right = after[ROWS : ROWS + 1, : 2 * 16].astype(jnp.int32)
    return last_update(notes_left, notes_right, partly, from_left, from_right)


def solution(mesh):
    placed = (
        P(),
        P(),
        P("slab", "scan", None, None),
        P("scan", None, None, None, None),
        P("scan", None, None),
        P("scan", None, None),
    )
    return jax.shard_map(
        shards, mesh=mesh, in_specs=placed, out_specs=P("slab", "scan", None, None), check_vma=False
    )
```

```python
import functools

import jax
import jax.numpy as jnp
from jax import lax
from jax.experimental import pallas as pl
from jax.experimental.pallas import tpu as pltpu
from jax.sharding import PartitionSpec as P

step_rate = 0.125
F32, BF16 = jnp.float32, jnp.bfloat16
NP, TS, HALF = 256, 128, 15
MODES, POS, CAP = 4, 2, 8
STEP = 32
ROWS = CAP * TS
SMEM = pl.BlockSpec(memory_space=pltpu.SMEM)
VMEM = pl.BlockSpec(memory_space=pltpu.VMEM)
HBM = pl.BlockSpec(memory_space=pltpu.HBM)


def params(mib):
    return pltpu.CompilerParams(vmem_limit_bytes=mib * 1024 * 1024)


def dot(left, right):
    return jnp.dot(left, right, preferred_element_type=F32)


def lanes(rows):
    return lax.broadcasted_iota(jnp.int32, (rows, TS), 1)


def pack_kernel(owners_hbm, offsets_hbm, tiles_hbm, out, owners, offsets, tiles, small, large):
    copies = [pltpu.make_async_copy(tiles_hbm.at[0, q], tiles.at[q], large.at[q]) for q in range(CAP)]
    for copy in copies:
        copy.start()
    notes_in = [
        pltpu.make_async_copy(owners_hbm, owners, small.at[0]),
        pltpu.make_async_copy(offsets_hbm, offsets, small.at[1]),
    ]
    for copy in notes_in:
        copy.start()
    for q in range(CAP):
        copies[q].wait()
        out[q * TS : (q + 1) * TS, :] = tiles[q].astype(BF16)
    for copy in notes_in:
        copy.wait()
    spot = lax.broadcasted_iota(jnp.int32, (16, 2 * TS), 1)
    notes = jnp.zeros((16, 2 * TS), jnp.int32)
    for p in range(POS):
        for k in range(9):
            notes = jnp.where(spot == p * 16 + k, owners[0, p, k] & (CAP - 1), notes)
        notes = jnp.where(spot == p * 16 + 9, offsets[0, p, 0], notes)
    out[ROWS : ROWS + 16, :] = notes.astype(F32).astype(BF16)


def pack(owners, offsets, tiles):
    return pl.pallas_call(
        pack_kernel,
        out_shape=jax.ShapeDtypeStruct((ROWS + 16, 2 * TS), BF16),
        in_specs=[HBM] * 3,
        out_specs=VMEM,
        scratch_shapes=[
            pltpu.SMEM(owners.shape, jnp.int32),
            pltpu.SMEM(offsets.shape, jnp.int32),
            pltpu.VMEM((CAP, TS, 2 * TS), F32),
            pltpu.SemaphoreType.DMA((2,)),
            pltpu.SemaphoreType.DMA((CAP,)),
        ],
        compiler_params=params(62),
        name="pack_tiles",
    )(owners, offsets, tiles)


def band(taps, row):
    wide = jnp.broadcast_to(taps[row : row + 1, :], (NP, NP))
    turned = pltpu.roll(wide, NP - HALF, 1, stride=1, stride_axis=0)
    gap = lax.broadcasted_iota(jnp.int32, (NP, NP), 1) - lax.broadcasted_iota(jnp.int32, (NP, NP), 0)
    return jnp.where(jnp.abs(gap) <= HALF, turned, 0.0)


def exit_kernel(taps, residual, left, left_adj, right, right_adj, wave, line):
    line[...] = jnp.zeros_like(line)
    for row in range(4):
        line[row : row + 1, 0 : 2 * HALF + 1] = taps[row // 2, row % 2 : row % 2 + 1, :].astype(F32)
    values = line[...]
    for first, plain, adj in ((0, left, left_adj), (2, right_adj, right)):
        re, im = band(values, first), band(values, first + 1)
        ret, imt = re.T, im.T
        plain[0:NP, 0:NP] = re.astype(BF16)
        plain[0:NP, NP:] = (-im).astype(BF16)
        plain[NP:, 0:NP] = im.astype(BF16)
        plain[NP:, NP:] = re.astype(BF16)
        adj[0:NP, 0:NP] = ret.astype(BF16)
        adj[0:NP, NP:] = imt.astype(BF16)
        adj[NP:, 0:NP] = (-imt).astype(BF16)
        adj[NP:, NP:] = ret.astype(BF16)
    for m in range(MODES):
        w = dot(residual[0, 0, m], right_adj[...]).astype(BF16)
        w = jnp.concatenate([w[:, :NP], w[:, NP:]], 0)
        wave[m] = dot(left_adj[...], w).astype(BF16)


def exit_adjoint(side, taps, residual):
    whole = lambda *shape: pl.BlockSpec(shape, lambda i, side: (0,) * len(shape))
    return pl.pallas_call(
        lambda side, *refs: exit_kernel(*refs),
        grid_spec=pltpu.PrefetchScalarGridSpec(
            num_scalar_prefetch=1,
            grid=(1,),
            in_specs=[
                whole(2, 2, 2 * HALF + 1),
                pl.BlockSpec((1, 1, MODES, NP, 2 * NP), lambda i, side: (0, side[0], 0, 0, 0)),
            ],
            out_specs=[whole(2 * NP, 2 * NP)] * 4 + [whole(MODES, 2 * NP, NP)],
            scratch_shapes=[pltpu.VMEM((8, NP), F32)],
        ),
        out_shape=[jax.ShapeDtypeStruct((2 * NP, 2 * NP), BF16)] * 4
        + [jax.ShapeDtypeStruct((MODES, 2 * NP, NP), BF16)],
        compiler_params=params(24),
        cost_estimate=pl.CostEstimate(flops=1_100_000_000, bytes_accessed=6_000_000, transcendentals=0),
        name="exit_adjoint",
    )(side, taps, residual)


def early_side():
    return 1 - lax.axis_index("scan") % 2


def cut_column(p, j, owners, offsets, tiles, stack, put):
    for i in range(3):
        q = owners[0, p, 3 * i + j] & (CAP - 1)
        tile = tiles[pl.ds(pl.multiple_of(q * TS, TS), TS), :].astype(F32)
        stack[0, i * TS : (i + 1) * TS, :] = tile[:, :TS]
        stack[1, i * TS : (i + 1) * TS, :] = tile[:, TS:]
    r, c = offsets[0, p, 0], offsets[0, p, 1]
    back = (TS - c) & (TS - 1)
    for at in range(0, NP, STEP):
        for part in range(2):
            put(part, at, pltpu.roll(stack[part, pl.ds(r + at, STEP), :], back, 1))


def half(side):
    return pl.ds(pl.multiple_of(side * TS, TS), TS)


def taken(side, c):
    past = lanes(STEP) - (TS - c)
    return past * (1 - 2 * side) - side < 0


def early_kernel(owners, offsets, own, early, out, stack):
    side = early_side()
    for p in range(POS):

        def put_own(part, at, turned):
            out[p, part, at : at + STEP, :TS] = turned
            out[p, part, at : at + STEP, TS:] = turned

        cut_column(p, 1, owners, offsets, own, stack.at[0], put_own)
        mask = taken(side, offsets[0, p, 1])

        def put_early(part, at, turned):
            place = (p, part, slice(at, at + STEP), half(side))
            out[place] = jnp.where(mask, turned, out[place])

        cut_column(p, 2 * side, owners, offsets, early, stack.at[1], put_early)


def early_windows(owners, offsets, own, early):
    return pl.pallas_call(
        early_kernel,
        out_shape=jax.ShapeDtypeStruct((POS, 2, NP, NP), F32),
        in_specs=[SMEM, SMEM, VMEM, VMEM],
        out_specs=VMEM,
        scratch_shapes=[pltpu.VMEM((2, 2, 3 * TS, TS), F32)],
        compiler_params=params(8),
        cost_estimate=pl.CostEstimate(flops=2_000_000, bytes_accessed=2_000_000, transcendentals=0),
        name="early_windows",
    )(owners, offsets, own, early)


def complete(p, owners, offsets, late, partly, stack, out):
    side = 1 - early_side()
    mask = taken(side, offsets[0, p, 1])

    def put(part, at, turned):
        rows = slice(at, at + STEP)
        kept = partly[p, part, rows, half(side)]
        out[part, rows, half(side)] = jnp.where(mask, turned, kept).astype(out.dtype)
        out[part, rows, half(1 - side)] = partly[p, part, rows, half(1 - side)].astype(out.dtype)

    cut_column(p, 2 * side, owners, offsets, late, stack, put)


def window_kernel(owners, offsets, late, partly, out, stack):
    complete(1 - lax.axis_index("slab"), owners, offsets, late, partly, stack, out)


def far_window(owners, offsets, late, partly):
    return pl.pallas_call(
        window_kernel,
        out_shape=jax.ShapeDtypeStruct((2, NP, NP), BF16),
        in_specs=[SMEM, SMEM, VMEM, VMEM],
        out_specs=VMEM,
        scratch_shapes=[pltpu.VMEM((2, 3 * TS, TS), F32)],
        compiler_params=params(8),
        cost_estimate=pl.CostEstimate(flops=1_000_000, bytes_accessed=2_000_000, transcendentals=0),
        name="far_window",
    )(owners, offsets, late, partly)


def times(a, b, conjugate):
    (ar, ai), (br, bi) = a, b
    if conjugate:
        return ar * br + ai * bi, ar * bi - ai * br
    return ar * br - ai * bi, ar * bi + ai * br


def beside(ref, m):
    return ref[m, :, :NP].astype(F32), ref[m, :, NP:].astype(F32)


def above(ref, m):
    return ref[m, :NP, :].astype(F32), ref[m, NP:, :].astype(F32)


def lower_terms(t, probe, wave, left, right, total):
    for m in range(MODES):
        window = (t[0].astype(F32), t[1].astype(F32))
        u = jnp.concatenate(times(beside(probe, m), window, False), 0).astype(BF16)
        v = dot(left[...], u).astype(BF16)
        v = jnp.concatenate([v[:NP], v[NP:]], 1)
        psi = dot(v, right[...]).astype(BF16).astype(F32)
        re, im = times((psi[:, :NP], psi[:, NP:]), above(wave, m), True)
        if m == 0:
            total[0], total[1] = re, im
        else:
            total[0] += re
            total[1] += im


def upper_terms(t, probe, wave, left_adj, right_adj, total):
    for m in range(MODES):
        window = (t[0].astype(F32), t[1].astype(F32))
        b = jnp.concatenate(times(window, above(wave, m), True), 1).astype(BF16)
        w = dot(b, right_adj[...]).astype(BF16)
        w = jnp.concatenate([w[:, :NP], w[:, NP:]], 0)
        a = dot(left_adj[...], w).astype(BF16).astype(F32)
        re, im = times(beside(probe, m), (a[:NP], a[NP:]), True)
        if m == 0:
            total[0], total[1] = re, im
        else:
            total[0] += re
            total[1] += im


def both_ways(chosen, t, probe, wave, left, left_adj, right, right_adj, total):
    @pl.when(chosen == 0)
    def _():
        lower_terms(t, probe, wave, left, right, total)

    @pl.when(chosen == 1)
    def _():
        upper_terms(t, probe, wave, left_adj, right_adj, total)


def near_kernel(owners, offsets, late, partly, probe, wave, left, left_adj, right, right_adj, out, stack, t, total):
    side = lax.axis_index("slab")
    complete(side, owners, offsets, late, partly, stack, t)
    both_ways(side, t, probe, wave, left, left_adj, right, right_adj, total)
    out[...] = total[...].astype(BF16)


def far_kernel(t, probe, wave, left, left_adj, right, right_adj, out):
    side = lax.axis_index("slab")
    both_ways(1 - side, t, probe, wave, left, left_adj, right, right_adj, out)


COST = pl.CostEstimate(flops=1_100_000_000, bytes_accessed=5_000_000, transcendentals=0)


def near_terms(owners, offsets, late, partly, probe, wave, mats):
    return pl.pallas_call(
        near_kernel,
        out_shape=jax.ShapeDtypeStruct((2, NP, NP), BF16),
        in_specs=[SMEM, SMEM] + [VMEM] * 8,
        out_specs=VMEM,
        scratch_shapes=[
            pltpu.VMEM((2, 3 * TS, TS), F32),
            pltpu.VMEM((2, NP, NP), F32),
            pltpu.VMEM((2, NP, NP), F32),
        ],
        compiler_params=params(24),
        cost_estimate=COST,
        name="near_terms",
    )(owners, offsets, late, partly, probe, wave, *mats)


def far_terms(t, probe, wave, mats):
    return pl.pallas_call(
        far_kernel,
        out_shape=jax.ShapeDtypeStruct((2, NP, NP), F32),
        in_specs=[VMEM] * 7,
        out_specs=VMEM,
        compiler_params=params(24),
        cost_estimate=COST,
        name="far_terms",
    )(t, probe, wave, *mats)


def split_kernel(offsets, mine, others, early, own, late):
    here = lax.axis_index("slab")
    to_right = early_side() == 1
    spot = lanes(STEP)
    for k, terms in ((0, mine), (1, others)):
        p = here if k == 0 else 1 - here
        c = offsets[0, p, 1]
        for at in range(0, NP, STEP):
            for part in range(2):
                low = pltpu.roll(terms[part, at : at + STEP, 0:TS].astype(F32), c, 1)
                high = pltpu.roll(terms[part, at : at + STEP, TS:].astype(F32), c, 1)
                place = (pl.ds(p * NP + at, STEP), slice(part * TS, (part + 1) * TS))
                left = jnp.where(spot >= c, low, 0.0)
                right = jnp.where(spot < c, high, 0.0)
                own[place] = jnp.where(spot < c, low, high)
                early[place] = jnp.where(to_right, right, left).astype(BF16)
                late[place] = jnp.where(to_right, left, right).astype(BF16)


def split_terms(offsets, mine, others):
    shape = (POS * NP, 2 * TS)
    return pl.pallas_call(
        split_kernel,
        out_shape=[
            jax.ShapeDtypeStruct(shape, BF16),
            jax.ShapeDtypeStruct(shape, F32),
            jax.ShapeDtypeStruct(shape, BF16),
        ],
        in_specs=[SMEM, VMEM, VMEM],
        out_specs=[VMEM] * 3,
        compiler_params=params(8),
        name="split_terms",
    )(offsets, mine, others)


def take_off(terms, slot, row, stack, out):
    for p in range(POS):
        for part in range(2):
            cols = slice(part * TS, (part + 1) * TS)
            stack[part, TS : TS + NP, :] = terms[p * NP : (p + 1) * NP, cols].astype(F32) * step_rate
        r = row(p)
        for i in range(3):
            for part in range(2):
                cols = slice(part * TS, (part + 1) * TS)
                out[0, slot(p, i), :, cols] -= stack[part, pl.ds(TS + i * TS - r, TS), :]


def clear(stack):
    stack[:, 0:TS, :] = jnp.zeros((2, TS, TS), F32)
    stack[:, TS + NP :, :] = jnp.zeros((2, TS, TS), F32)


def own_kernel(owners, offsets, tiles, terms, out, stack):
    clear(stack)
    out[...] = tiles[...]
    take_off(terms, lambda p, i: owners[0, p, 3 * i + 1] & (CAP - 1), lambda p: offsets[0, p, 0], stack, out)


def own_update(owners, offsets, tiles, terms):
    return pl.pallas_call(
        own_kernel,
        out_shape=jax.ShapeDtypeStruct(tiles.shape, F32),
        in_specs=[SMEM, SMEM, VMEM, VMEM],
        out_specs=VMEM,
        scratch_shapes=[pltpu.VMEM((2, 2 * TS + NP, TS), F32)],
        compiler_params=params(8),
        cost_estimate=pl.CostEstimate(flops=1_000_000, bytes_accessed=3_000_000, transcendentals=0),
        name="own_update",
    )(owners, offsets, tiles, terms)


def early_update_kernel(notes, tiles, terms, out, stack):
    clear(stack)
    j = 2 - 2 * early_side()
    out[...] = tiles[...]
    take_off(terms, lambda p, i: notes[0, p * 16 + 3 * i + j], lambda p: notes[0, p * 16 + 9], stack, out)


def late_update_kernel(notes, tiles, terms, out, stack):
    clear(stack)
    j = 2 * early_side()
    out[...] = tiles[...]
    take_off(terms, lambda p, i: notes[0, p * 16 + 3 * i + j], lambda p: notes[0, p * 16 + 9], stack, out)


def swap_update(kernel, notes, tiles, terms):
    return pl.pallas_call(
        kernel,
        out_shape=jax.ShapeDtypeStruct(tiles.shape, F32),
        in_specs=[SMEM, VMEM, VMEM],
        out_specs=VMEM,
        scratch_shapes=[pltpu.VMEM((2, 2 * TS + NP, TS), F32)],
        compiler_params=params(8),
        cost_estimate=pl.CostEstimate(flops=1_000_000, bytes_accessed=3_000_000, transcendentals=0),
        name="swap_update",
    )(notes, tiles, terms)


def swap(value, first):
    count = lax.axis_size("scan")
    pairs = [(i, (i + 1) % count) for i in range(first, count, 2)]
    return lax.ppermute(value, "scan", pairs + [(j, i) for i, j in pairs])


def across(value):
    return lax.ppermute(value, "slab", [(0, 1), (1, 0)])


def notes_of(packed):
    return packed[ROWS : ROWS + 1, : 2 * 16].astype(jnp.int32)


def shards(probe_modes, tap_weights, object_slices, exit_residual, offsets, owners):
    side = lax.axis_index("slab").astype(jnp.int32).reshape(1)
    own = pack(owners, offsets, object_slices)
    late = swap(own, 1)
    early = swap(own, 0)
    *mats, wave = exit_adjoint(side, tap_weights, exit_residual)
    partly = early_windows(owners, offsets, own, early)
    t_there = far_window(owners, offsets, late, partly)
    t_here = across(t_there)
    terms_there = near_terms(owners, offsets, late, partly, probe_modes, wave, mats)
    terms_far = across(terms_there)
    terms_here = far_terms(t_here, probe_modes, wave, mats)
    early_out, kept, late_out = split_terms(offsets, terms_here, terms_far)
    late_in = swap(late_out, 1)
    early_in = swap(early_out, 0)
    tiles = own_update(owners, offsets, object_slices, kept)
    tiles = swap_update(early_update_kernel, notes_of(early), tiles, early_in)
    return swap_update(late_update_kernel, notes_of(late), tiles, late_in)


def solution(mesh):
    placed = (
        P(),
        P(),
        P("slab", "scan", None, None),
        P("scan", None, None, None, None),
        P("scan", None, None),
        P("scan", None, None),
    )
    return jax.shard_map(
        shards, mesh=mesh, in_specs=placed, out_specs=P("slab", "scan", None, None), check_vma=False
    )
```

```python
import functools

import jax
import jax.numpy as jnp
from jax import lax
from jax.experimental import pallas as pl
from jax.experimental.pallas import tpu as pltpu
from jax.sharding import PartitionSpec as P

step_rate = 0.125
F32, BF16 = jnp.float32, jnp.bfloat16
NP, TS, HALF = 256, 128, 15
MODES, POS, CAP = 4, 2, 8
STEP = 32
SMEM = pl.BlockSpec(memory_space=pltpu.SMEM)
VMEM = pl.BlockSpec(memory_space=pltpu.VMEM)
HBM = pl.BlockSpec(memory_space=pltpu.HBM)


def params(mib):
    return pltpu.CompilerParams(vmem_limit_bytes=mib * 1024 * 1024)


def dot(left, right):
    return jnp.dot(left, right, preferred_element_type=F32)


def lanes(rows):
    return lax.broadcasted_iota(jnp.int32, (rows, TS), 1)


def band(taps, row):
    wide = jnp.broadcast_to(taps[row : row + 1, :], (NP, NP))
    turned = pltpu.roll(wide, NP - HALF, 1, stride=1, stride_axis=0)
    gap = lax.broadcasted_iota(jnp.int32, (NP, NP), 1) - lax.broadcasted_iota(jnp.int32, (NP, NP), 0)
    return jnp.where(jnp.abs(gap) <= HALF, turned, 0.0)


def exit_kernel(taps, residual, left, left_adj, right, right_adj, wave, line):
    line[...] = jnp.zeros_like(line)
    for row in range(4):
        line[row : row + 1, 0 : 2 * HALF + 1] = taps[row // 2, row % 2 : row % 2 + 1, :].astype(F32)
    values = line[...]
    for first, plain, adj in ((0, left, left_adj), (2, right_adj, right)):
        re, im = band(values, first), band(values, first + 1)
        ret, imt = re.T, im.T
        plain[0:NP, 0:NP] = re.astype(BF16)
        plain[0:NP, NP:] = (-im).astype(BF16)
        plain[NP:, 0:NP] = im.astype(BF16)
        plain[NP:, NP:] = re.astype(BF16)
        adj[0:NP, 0:NP] = ret.astype(BF16)
        adj[0:NP, NP:] = imt.astype(BF16)
        adj[NP:, 0:NP] = (-imt).astype(BF16)
        adj[NP:, NP:] = ret.astype(BF16)
    for m in range(MODES):
        w = dot(residual[0, 0, m], right_adj[...]).astype(BF16)
        w = jnp.concatenate([w[:, :NP], w[:, NP:]], 0)
        wave[m] = dot(left_adj[...], w).astype(BF16)


def exit_adjoint(side, taps, residual):
    whole = lambda *shape: pl.BlockSpec(shape, lambda i, side: (0,) * len(shape))
    return pl.pallas_call(
        lambda side, *refs: exit_kernel(*refs),
        grid_spec=pltpu.PrefetchScalarGridSpec(
            num_scalar_prefetch=1,
            grid=(1,),
            in_specs=[
                whole(2, 2, 2 * HALF + 1),
                pl.BlockSpec((1, 1, MODES, NP, 2 * NP), lambda i, side: (0, side[0], 0, 0, 0)),
            ],
            out_specs=[whole(2 * NP, 2 * NP)] * 4 + [whole(MODES, 2 * NP, NP)],
            scratch_shapes=[pltpu.VMEM((8, NP), F32)],
        ),
        out_shape=[jax.ShapeDtypeStruct((2 * NP, 2 * NP), BF16)] * 4
        + [jax.ShapeDtypeStruct((MODES, 2 * NP, NP), BF16)],
        compiler_params=params(24),
        cost_estimate=pl.CostEstimate(flops=1_100_000_000, bytes_accessed=6_000_000, transcendentals=0),
        name="exit_adjoint",
    )(side, taps, residual)


def early_side():
    return 1 - lax.axis_index("scan") % 2


def packed_tile(tiles):
    return lambda q: tiles[q].astype(F32)


def plain_tile(tiles):
    return lambda q: tiles[0, q].astype(BF16).astype(F32)


def cut_column(p, j, owners, offsets, tile_at, stack, put):
    for i in range(3):
        tile = tile_at(owners[0, p, 3 * i + j] & (CAP - 1))
        stack[0, i * TS : (i + 1) * TS, :] = tile[:, :TS]
        stack[1, i * TS : (i + 1) * TS, :] = tile[:, TS:]
    r, c = offsets[0, p, 0], offsets[0, p, 1]
    back = (TS - c) & (TS - 1)
    for at in range(0, NP, STEP):
        for part in range(2):
            put(part, at, pltpu.roll(stack[part, pl.ds(r + at, STEP), :], back, 1))


def half(side):
    return pl.ds(pl.multiple_of(side * TS, TS), TS)


def taken(side, c):
    past = lanes(STEP) - (TS - c)
    return past * (1 - 2 * side) - side < 0


def early_kernel(owners, offsets, own, early, out, stack):
    side = early_side()
    for p in range(POS):

        def put_own(part, at, turned):
            out[p, part, at : at + STEP, :TS] = turned
            out[p, part, at : at + STEP, TS:] = turned

        cut_column(p, 1, owners, offsets, plain_tile(own), stack.at[0], put_own)
        mask = taken(side, offsets[0, p, 1])

        def put_early(part, at, turned):
            place = (p, part, slice(at, at + STEP), half(side))
            out[place] = jnp.where(mask, turned, out[place])

        cut_column(p, 2 * side, owners, offsets, packed_tile(early), stack.at[1], put_early)


def early_windows(owners, offsets, own, early):
    return pl.pallas_call(
        early_kernel,
        out_shape=jax.ShapeDtypeStruct((POS, 2, NP, NP), F32),
        in_specs=[SMEM, SMEM, VMEM, VMEM],
        out_specs=VMEM,
        scratch_shapes=[pltpu.VMEM((2, 2, 3 * TS, TS), F32)],
        compiler_params=params(8),
        cost_estimate=pl.CostEstimate(flops=2_000_000, bytes_accessed=2_000_000, transcendentals=0),
        name="early_windows",
    )(owners, offsets, own, early)


def complete(p, owners, offsets, late, partly, stack, out):
    side = 1 - early_side()
    mask = taken(side, offsets[0, p, 1])

    def put(part, at, turned):
        rows = slice(at, at + STEP)
        kept = partly[p, part, rows, half(side)]
        out[part, rows, half(side)] = jnp.where(mask, turned, kept).astype(out.dtype)
        out[part, rows, half(1 - side)] = partly[p, part, rows, half(1 - side)].astype(out.dtype)

    cut_column(p, 2 * side, owners, offsets, packed_tile(late), stack, put)


def late_kernel(owners, offsets, late, partly, far, near, stack):
    here = lax.axis_index("slab")
    complete(1 - here, owners, offsets, late, partly, stack.at[0], far)
    complete(here, owners, offsets, late, partly, stack.at[1], near)


def late_windows(owners, offsets, late, partly):
    return pl.pallas_call(
        late_kernel,
        out_shape=[jax.ShapeDtypeStruct((2, NP, NP), BF16)] * 2,
        in_specs=[SMEM, SMEM, VMEM, VMEM],
        out_specs=[VMEM] * 2,
        scratch_shapes=[pltpu.VMEM((2, 2, 3 * TS, TS), F32)],
        compiler_params=params(8),
        cost_estimate=pl.CostEstimate(flops=1_000_000, bytes_accessed=2_000_000, transcendentals=0),
        name="late_windows",
    )(owners, offsets, late, partly)


def times(a, b, conjugate):
    (ar, ai), (br, bi) = a, b
    if conjugate:
        return ar * br + ai * bi, ar * bi - ai * br
    return ar * br - ai * bi, ar * bi + ai * br


def beside(ref, m):
    return ref[m, :, :NP].astype(F32), ref[m, :, NP:].astype(F32)


def above(ref, m):
    return ref[m, :NP, :].astype(F32), ref[m, NP:, :].astype(F32)


def lower_terms(t, probe, wave, left, right, total):
    for m in range(MODES):
        window = (t[0].astype(F32), t[1].astype(F32))
        u = jnp.concatenate(times(beside(probe, m), window, False), 0).astype(BF16)
        v = dot(left[...], u).astype(BF16)
        v = jnp.concatenate([v[:NP], v[NP:]], 1)
        psi = dot(v, right[...]).astype(BF16).astype(F32)
        re, im = times((psi[:, :NP], psi[:, NP:]), above(wave, m), True)
        if m == 0:
            total[0], total[1] = re, im
        else:
            total[0] += re
            total[1] += im


def upper_terms(t, probe, wave, left_adj, right_adj, total):
    for m in range(MODES):
        window = (t[0].astype(F32), t[1].astype(F32))
        b = jnp.concatenate(times(window, above(wave, m), True), 1).astype(BF16)
        w = dot(b, right_adj[...]).astype(BF16)
        w = jnp.concatenate([w[:, :NP], w[:, NP:]], 0)
        a = dot(left_adj[...], w).astype(BF16).astype(F32)
        re, im = times(beside(probe, m), (a[:NP], a[NP:]), True)
        if m == 0:
            total[0], total[1] = re, im
        else:
            total[0] += re
            total[1] += im


def both_ways(chosen, t, probe, wave, left, left_adj, right, right_adj, total):
    @pl.when(chosen == 0)
    def _():
        lower_terms(t, probe, wave, left, right, total)

    @pl.when(chosen == 1)
    def _():
        upper_terms(t, probe, wave, left_adj, right_adj, total)


def near_kernel(t, probe, wave, left, left_adj, right, right_adj, out, total):
    side = lax.axis_index("slab")
    both_ways(side, t, probe, wave, left, left_adj, right, right_adj, total)
    out[...] = total[...].astype(BF16)


def far_kernel(t, probe, wave, left, left_adj, right, right_adj, out):
    side = lax.axis_index("slab")
    both_ways(1 - side, t, probe, wave, left, left_adj, right, right_adj, out)


COST = pl.CostEstimate(flops=1_100_000_000, bytes_accessed=5_000_000, transcendentals=0)


def near_terms(t, probe, wave, mats):
    return pl.pallas_call(
        near_kernel,
        out_shape=jax.ShapeDtypeStruct((2, NP, NP), BF16),
        in_specs=[VMEM] * 7,
        out_specs=VMEM,
        scratch_shapes=[pltpu.VMEM((2, NP, NP), F32)],
        compiler_params=params(24),
        cost_estimate=COST,
        name="near_terms",
    )(t, probe, wave, *mats)


def far_terms(t, probe, wave, mats):
    return pl.pallas_call(
        far_kernel,
        out_shape=jax.ShapeDtypeStruct((2, NP, NP), F32),
        in_specs=[VMEM] * 7,
        out_specs=VMEM,
        compiler_params=params(24),
        cost_estimate=COST,
        name="far_terms",
    )(t, probe, wave, *mats)


def split_kernel(owners, offsets, mine, others, early, own, late):
    here = lax.axis_index("slab")
    place = lax.broadcasted_iota(jnp.int32, (16, 2 * TS), 1)
    notes = jnp.zeros((16, 2 * TS), jnp.int32)
    for p in range(POS):
        for k in range(9):
            notes = jnp.where(place == p * 16 + k, owners[0, p, k] & (CAP - 1), notes)
        notes = jnp.where(place == p * 16 + 9, offsets[0, p, 0], notes)
    early[POS * NP :, :] = notes.astype(F32).astype(BF16)
    late[POS * NP :, :] = notes.astype(F32).astype(BF16)
    to_right = early_side() == 1
    spot = lanes(STEP)
    for k, terms in ((0, mine), (1, others)):
        p = here if k == 0 else 1 - here
        c = offsets[0, p, 1]
        for at in range(0, NP, STEP):
            for part in range(2):
                low = pltpu.roll(terms[part, at : at + STEP, 0:TS].astype(F32), c, 1)
                high = pltpu.roll(terms[part, at : at + STEP, TS:].astype(F32), c, 1)
                place = (pl.ds(p * NP + at, STEP), slice(part * TS, (part + 1) * TS))
                left = jnp.where(spot >= c, low, 0.0)
                right = jnp.where(spot < c, high, 0.0)
                own[place] = jnp.where(spot < c, low, high)
                early[place] = jnp.where(to_right, right, left).astype(BF16)
                late[place] = jnp.where(to_right, left, right).astype(BF16)


def split_terms(owners, offsets, mine, others):
    sent = jax.ShapeDtypeStruct((POS * NP + 16, 2 * TS), BF16)
    return pl.pallas_call(
        split_kernel,
        out_shape=[sent, jax.ShapeDtypeStruct((POS * NP, 2 * TS), F32), sent],
        in_specs=[SMEM, SMEM, VMEM, VMEM],
        out_specs=[VMEM] * 3,
        compiler_params=params(8),
        name="split_terms",
    )(owners, offsets, mine, others)


STACK = pltpu.VMEM((POS, 2, 2 * TS + NP, TS), F32)


def fill(terms, stack):
    for p in range(POS):
        for part in range(2):
            cols = slice(part * TS, (part + 1) * TS)
            stack[p, part, :TS, :] = jnp.zeros((TS, TS), F32)
            stack[p, part, TS : TS + NP, :] = terms[p * NP : (p + 1) * NP, cols].astype(F32) * step_rate
            stack[p, part, TS + NP :, :] = jnp.zeros((TS, TS), F32)


def take_off(slots, rows, stack, tiles, done):
    for q in range(CAP):
        starts = []
        for p in range(POS):
            start = jnp.int32(0)
            for i in range(3):
                start = jnp.where(slots[p][i] == q, TS + i * TS - rows[p], start)
            starts.append(start)
        for part in range(2):
            tile = tiles[0, q, :, part * TS : (part + 1) * TS]
            for p in range(POS):
                tile = tile - stack[p, part, pl.ds(starts[p], TS), :]
            done(q, part, tile)


def keep(out):
    def done(q, part, tile):
        out[0, q, :, part * TS : (part + 1) * TS] = tile

    return done


def own_kernel(owners, offsets, tiles, terms, out, stack):
    slots = [[owners[0, p, 3 * i + 1] & (CAP - 1) for i in range(3)] for p in range(POS)]
    fill(terms, stack)
    take_off(slots, [offsets[0, p, 0] for p in range(POS)], stack, tiles, keep(out))


def own_update(owners, offsets, tiles, terms):
    return pl.pallas_call(
        own_kernel,
        out_shape=jax.ShapeDtypeStruct(tiles.shape, F32),
        in_specs=[SMEM, SMEM, VMEM, VMEM],
        out_specs=VMEM,
        scratch_shapes=[STACK],
        compiler_params=params(8),
        cost_estimate=pl.CostEstimate(flops=1_000_000, bytes_accessed=3_000_000, transcendentals=0),
        name="own_update",
    )(owners, offsets, tiles, terms)


def read_notes(j, terms, lines, notes, sem):
    lines[...] = terms[POS * NP :, :TS].astype(F32).astype(jnp.int32)
    copy = pltpu.make_async_copy(lines.at[0:1], notes, sem)
    copy.start()
    return copy


def noted(j, notes):
    slots = [[notes[0, p * 16 + 3 * i + j] for i in range(3)] for p in range(POS)]
    return slots, [notes[0, p * 16 + 9] for p in range(POS)]


NOTES = [STACK, pltpu.VMEM((16, TS), jnp.int32), pltpu.SMEM((1, TS), jnp.int32), pltpu.SemaphoreType.DMA(())]


def early_update_kernel(tiles, terms, out, stack, lines, notes, sem):
    j = 2 - 2 * early_side()
    copy = read_notes(j, terms, lines, notes, sem)
    fill(terms, stack)
    copy.wait()
    take_off(*noted(j, notes), stack, tiles, keep(out))


def early_update(tiles, terms):
    return pl.pallas_call(
        early_update_kernel,
        out_shape=jax.ShapeDtypeStruct(tiles.shape, F32),
        in_specs=[VMEM, VMEM],
        out_specs=VMEM,
        scratch_shapes=NOTES,
        compiler_params=params(8),
        cost_estimate=pl.CostEstimate(flops=1_000_000, bytes_accessed=3_000_000, transcendentals=0),
        name="early_update",
    )(tiles, terms)


def late_update_kernel(tiles, terms, out, stack, lines, notes, sem, work, sems):
    j = 2 * early_side()
    copy = read_notes(j, terms, lines, notes, sem)
    fill(terms, stack)
    copy.wait()
    copies = [pltpu.make_async_copy(work.at[0, q], out.at[0, q], sems.at[q]) for q in range(CAP)]

    def done(q, part, tile):
        keep(work)(q, part, tile)
        if part == 1:
            copies[q].start()

    take_off(*noted(j, notes), stack, tiles, done)
    for copy in copies:
        copy.wait()


def late_update(tiles, terms):
    return pl.pallas_call(
        late_update_kernel,
        out_shape=jax.ShapeDtypeStruct(tiles.shape, F32),
        in_specs=[VMEM, VMEM],
        out_specs=HBM,
        scratch_shapes=NOTES + [pltpu.VMEM((1, CAP, TS, 2 * TS), F32), pltpu.SemaphoreType.DMA((CAP,))],
        compiler_params=params(8),
        name="late_update",
    )(tiles, terms)


def swap(value, first):
    count = lax.axis_size("scan")
    pairs = [(i, (i + 1) % count) for i in range(first, count, 2)]
    return lax.ppermute(value, "scan", pairs + [(j, i) for i, j in pairs])


def across(value):
    return lax.ppermute(value, "slab", [(0, 1), (1, 0)])


def shards(probe_modes, tap_weights, object_slices, exit_residual, offsets, owners):
    side = lax.axis_index("slab").astype(jnp.int32).reshape(1)
    own = object_slices[0].astype(BF16)
    late = swap(own, 1)
    early = swap(own, 0)
    *mats, wave = exit_adjoint(side, tap_weights, exit_residual)
    partly = early_windows(owners, offsets, object_slices, early)
    t_there, t_near = late_windows(owners, offsets, late, partly)
    t_here = across(t_there)
    terms_there = near_terms(t_near, probe_modes, wave, mats)
    terms_far = across(terms_there)
    terms_here = far_terms(t_here, probe_modes, wave, mats)
    early_out, kept, late_out = split_terms(owners, offsets, terms_here, terms_far)
    late_in = swap(late_out, 1)
    early_in = swap(early_out, 0)
    tiles = own_update(owners, offsets, object_slices, kept)
    tiles = early_update(tiles, early_in)
    return late_update(tiles, late_in)


def solution(mesh):
    placed = (
        P(),
        P(),
        P("slab", "scan", None, None),
        P("scan", None, None, None, None),
        P("scan", None, None),
        P("scan", None, None),
    )
    return jax.shard_map(
        shards, mesh=mesh, in_specs=placed, out_specs=P("slab", "scan", None, None), check_vma=False
    )
```

```python
import functools

import jax
import jax.numpy as jnp
from jax import lax
from jax.experimental import pallas as pl
from jax.experimental.pallas import tpu as pltpu
from jax.sharding import PartitionSpec as P

step_rate = 0.125
F32, BF16 = jnp.float32, jnp.bfloat16
NP, TS, HALF = 256, 128, 15
MODES, POS, CAP = 4, 2, 8
STEP = 32
SMEM = pl.BlockSpec(memory_space=pltpu.SMEM)
VMEM = pl.BlockSpec(memory_space=pltpu.VMEM)
HBM = pl.BlockSpec(memory_space=pltpu.HBM)


def params(mib):
    return pltpu.CompilerParams(vmem_limit_bytes=mib * 1024 * 1024)


def dot(left, right):
    return jnp.dot(left, right, preferred_element_type=F32)


def lanes(rows):
    return lax.broadcasted_iota(jnp.int32, (rows, TS), 1)


def band(taps, row):
    wide = jnp.broadcast_to(taps[row : row + 1, :], (NP, NP))
    turned = pltpu.roll(wide, NP - HALF, 1, stride=1, stride_axis=0)
    gap = lax.broadcasted_iota(jnp.int32, (NP, NP), 1) - lax.broadcasted_iota(jnp.int32, (NP, NP), 0)
    return jnp.where(jnp.abs(gap) <= HALF, turned, 0.0)


def exit_kernel(taps, residual, left, left_adj, right, right_adj, wave, line):
    line[...] = jnp.zeros_like(line)
    for row in range(4):
        line[row : row + 1, 0 : 2 * HALF + 1] = taps[row // 2, row % 2 : row % 2 + 1, :].astype(F32)
    values = line[...]
    for first, plain, adj in ((0, left, left_adj), (2, right_adj, right)):
        re, im = band(values, first), band(values, first + 1)
        ret, imt = re.T, im.T
        plain[0:NP, 0:NP] = re.astype(BF16)
        plain[0:NP, NP:] = (-im).astype(BF16)
        plain[NP:, 0:NP] = im.astype(BF16)
        plain[NP:, NP:] = re.astype(BF16)
        adj[0:NP, 0:NP] = ret.astype(BF16)
        adj[0:NP, NP:] = imt.astype(BF16)
        adj[NP:, 0:NP] = (-imt).astype(BF16)
        adj[NP:, NP:] = ret.astype(BF16)
    for m in range(MODES):
        w = dot(residual[0, 0, m], right_adj[...]).astype(BF16)
        w = jnp.concatenate([w[:, :NP], w[:, NP:]], 0)
        wave[m] = dot(left_adj[...], w).astype(BF16)


def exit_adjoint(side, taps, residual):
    whole = lambda *shape: pl.BlockSpec(shape, lambda i, side: (0,) * len(shape))
    return pl.pallas_call(
        lambda side, *refs: exit_kernel(*refs),
        grid_spec=pltpu.PrefetchScalarGridSpec(
            num_scalar_prefetch=1,
            grid=(1,),
            in_specs=[
                whole(2, 2, 2 * HALF + 1),
                pl.BlockSpec((1, 1, MODES, NP, 2 * NP), lambda i, side: (0, side[0], 0, 0, 0)),
            ],
            out_specs=[whole(2 * NP, 2 * NP)] * 4 + [whole(MODES, 2 * NP, NP)],
            scratch_shapes=[pltpu.VMEM((8, NP), F32)],
        ),
        out_shape=[jax.ShapeDtypeStruct((2 * NP, 2 * NP), BF16)] * 4
        + [jax.ShapeDtypeStruct((MODES, 2 * NP, NP), BF16)],
        compiler_params=params(24),
        cost_estimate=pl.CostEstimate(flops=1_100_000_000, bytes_accessed=6_000_000, transcendentals=0),
        name="exit_adjoint",
    )(side, taps, residual)


FIRST, SECOND, THIRD = (0, 2, 4), (5, 7), (1, 3, 6)


def part_in(members):
    z = lax.axis_index("scan") % 8
    right = functools.reduce(jnp.logical_or, [z == i for i in members])
    left = functools.reduce(jnp.logical_or, [z == (i + 1) % 8 for i in members])
    return jnp.logical_or(left, right), right.astype(jnp.int32)


def early_side():
    return 1 - lax.axis_index("scan") % 2


def packed_tile(tiles):
    return lambda q: tiles[q].astype(F32)


def plain_tile(tiles):
    return lambda q: tiles[0, q].astype(BF16).astype(F32)


def cut_column(p, j, owners, offsets, tile_at, stack, put):
    for i in range(3):
        tile = tile_at(owners[0, p, 3 * i + j] & (CAP - 1))
        stack[0, i * TS : (i + 1) * TS, :] = tile[:, :TS]
        stack[1, i * TS : (i + 1) * TS, :] = tile[:, TS:]
    r, c = offsets[0, p, 0], offsets[0, p, 1]
    back = (TS - c) & (TS - 1)
    for at in range(0, NP, STEP):
        for part in range(2):
            put(part, at, pltpu.roll(stack[part, pl.ds(r + at, STEP), :], back, 1))


def half(side):
    return pl.ds(pl.multiple_of(side * TS, TS), TS)


def taken(side, c):
    past = lanes(STEP) - (TS - c)
    return past * (1 - 2 * side) - side < 0


def early_kernel(owners, offsets, own, first, out, stack):
    inside, side = part_in(FIRST)
    for p in range(POS):

        def put_own(part, at, turned):
            out[p, part, at : at + STEP, :TS] = turned
            out[p, part, at : at + STEP, TS:] = turned

        cut_column(p, 1, owners, offsets, plain_tile(own), stack.at[0], put_own)

    @pl.when(inside)
    def _():
        for p in range(POS):
            overlay(p, side, owners, offsets, first, stack.at[1], out.at[p], out.at[p])


def overlay(p, side, owners, offsets, tiles, stack, base, out):
    mask = taken(side, offsets[0, p, 1])

    def put(part, at, turned):
        place = (part, slice(at, at + STEP), half(side))
        out[place] = jnp.where(mask, turned, base[place]).astype(out.dtype)

    cut_column(p, 2 * side, owners, offsets, packed_tile(tiles), stack, put)


def early_windows(owners, offsets, own, first):
    return pl.pallas_call(
        early_kernel,
        out_shape=jax.ShapeDtypeStruct((POS, 2, NP, NP), F32),
        in_specs=[SMEM, SMEM, VMEM, VMEM],
        out_specs=VMEM,
        scratch_shapes=[pltpu.VMEM((2, 2, 3 * TS, TS), F32)],
        compiler_params=params(8),
        cost_estimate=pl.CostEstimate(flops=2_000_000, bytes_accessed=2_000_000, transcendentals=0),
        name="early_windows",
    )(owners, offsets, own, first)


def late_kernel(owners, offsets, third, second, partly, far, near, stack):
    here = lax.axis_index("slab")
    far[...] = partly[1 - here].astype(BF16)
    near[...] = partly[here].astype(BF16)
    for k, (members, tiles) in enumerate(((SECOND, second), (THIRD, third))):
        inside, side = part_in(members)

        @pl.when(inside)
        def _():
            for n, (p, out) in enumerate(((1 - here, far), (here, near))):
                overlay(p, side, owners, offsets, tiles, stack.at[2 * k + n], partly.at[p], out)


def late_windows(owners, offsets, second, third, partly):
    return pl.pallas_call(
        late_kernel,
        out_shape=[jax.ShapeDtypeStruct((2, NP, NP), BF16)] * 2,
        in_specs=[SMEM, SMEM, VMEM, VMEM, VMEM],
        out_specs=[VMEM] * 2,
        scratch_shapes=[pltpu.VMEM((4, 2, 3 * TS, TS), F32)],
        compiler_params=params(8),
        cost_estimate=pl.CostEstimate(flops=1_000_000, bytes_accessed=2_000_000, transcendentals=0),
        name="late_windows",
    )(owners, offsets, third, second, partly)


def times(a, b, conjugate):
    (ar, ai), (br, bi) = a, b
    if conjugate:
        return ar * br + ai * bi, ar * bi - ai * br
    return ar * br - ai * bi, ar * bi + ai * br


def beside(ref, m):
    return ref[m, :, :NP].astype(F32), ref[m, :, NP:].astype(F32)


def above(ref, m):
    return ref[m, :NP, :].astype(F32), ref[m, NP:, :].astype(F32)


def summed(pairs, total):
    for at in range(0, NP, STEP):
        rows = slice(at, at + STEP)
        re = im = None
        for left, right in pairs(rows):
            one_re, one_im = times(left, right, True)
            re, im = (one_re, one_im) if re is None else (re + one_re, im + one_im)
        total[0, rows, :], total[1, rows, :] = re.astype(total.dtype), im.astype(total.dtype)


def wide(ref, m, rows):
    return ref[m, rows, :NP].astype(F32), ref[m, rows, NP:].astype(F32)


def tall(ref, m, rows):
    return ref[m, rows, :].astype(F32), ref[m, slice(NP + rows.start, NP + rows.stop), :].astype(F32)


def lower_terms(t, probe, wave, left, right, total, rows_in, waves):
    window = (t[0].astype(F32), t[1].astype(F32))
    for m in range(MODES):
        u = jnp.concatenate(times(beside(probe, m), window, False), 0).astype(BF16)
        v = dot(left[...], u).astype(BF16)
        rows_in[m * NP : (m + 1) * NP, :NP] = v[:NP]
        rows_in[m * NP : (m + 1) * NP, NP:] = v[NP:]
    waves[...] = dot(rows_in[...], right[...]).reshape(MODES, NP, 2 * NP)
    summed(lambda rows: [(wide(waves, m, rows), tall(wave, m, rows)) for m in range(MODES)], total)


def upper_terms(t, probe, wave, left_adj, right_adj, total, rows_in, waves):
    window = (t[0].astype(F32), t[1].astype(F32))
    for m in range(MODES):
        re, im = times(window, above(wave, m), True)
        rows_in[m * NP : (m + 1) * NP, :NP] = re.astype(BF16)
        rows_in[m * NP : (m + 1) * NP, NP:] = im.astype(BF16)
    w = dot(rows_in[...], right_adj[...]).astype(BF16)
    for m in range(MODES):
        part = w[m * NP : (m + 1) * NP]
        waves[m] = dot(left_adj[...], jnp.concatenate([part[:, :NP], part[:, NP:]], 0))
    summed(lambda rows: [(wide(probe, m, rows), tall(waves, m, rows)) for m in range(MODES)], total)


def terms_kernel(far, t, probe, wave, left, left_adj, right, right_adj, out, rows_in, lower, upper):
    side = lax.axis_index("slab")
    chosen = 1 - side if far else side

    @pl.when(chosen == 0)
    def _():
        lower_terms(t, probe, wave, left, right, out, rows_in, lower)

    @pl.when(chosen == 1)
    def _():
        upper_terms(t, probe, wave, left_adj, right_adj, out, rows_in, upper)


def slice_terms(far, t, probe, wave, mats):
    return pl.pallas_call(
        functools.partial(terms_kernel, far),
        out_shape=jax.ShapeDtypeStruct((2, NP, NP), F32 if far else BF16),
        in_specs=[VMEM] * 7,
        out_specs=VMEM,
        scratch_shapes=[
            pltpu.VMEM((MODES * NP, 2 * NP), BF16),
            pltpu.VMEM((MODES, NP, 2 * NP), F32),
            pltpu.VMEM((MODES, 2 * NP, NP), F32),
        ],
        compiler_params=params(32),
        cost_estimate=pl.CostEstimate(flops=1_100_000_000, bytes_accessed=5_000_000, transcendentals=0),
        name="far_terms" if far else "near_terms",
    )(t, probe, wave, *mats)


def split_kernel(owners, offsets, mine, others, early, own, late):
    here = lax.axis_index("slab")
    place = lax.broadcasted_iota(jnp.int32, (16, 2 * TS), 1)
    notes = jnp.zeros((16, 2 * TS), jnp.int32)
    for p in range(POS):
        for k in range(9):
            notes = jnp.where(place == p * 16 + k, owners[0, p, k] & (CAP - 1), notes)
        notes = jnp.where(place == p * 16 + 9, offsets[0, p, 0], notes)
    early[POS * NP :, :] = notes.astype(F32).astype(BF16)
    late[POS * NP :, :] = notes.astype(F32).astype(BF16)
    to_right = early_side() == 1
    spot = lanes(STEP)
    for k, terms in ((0, mine), (1, others)):
        p = here if k == 0 else 1 - here
        c = offsets[0, p, 1]
        for at in range(0, NP, STEP):
            for part in range(2):
                low = pltpu.roll(terms[part, at : at + STEP, 0:TS].astype(F32), c, 1)
                high = pltpu.roll(terms[part, at : at + STEP, TS:].astype(F32), c, 1)
                place = (pl.ds(p * NP + at, STEP), slice(part * TS, (part + 1) * TS))
                left = jnp.where(spot >= c, low, 0.0)
                right = jnp.where(spot < c, high, 0.0)
                own[place] = jnp.where(spot < c, low, high)
                early[place] = jnp.where(to_right, right, left).astype(BF16)
                late[place] = jnp.where(to_right, left, right).astype(BF16)


def split_terms(owners, offsets, mine, others):
    sent = jax.ShapeDtypeStruct((POS * NP + 16, 2 * TS), BF16)
    return pl.pallas_call(
        split_kernel,
        out_shape=[sent, jax.ShapeDtypeStruct((POS * NP, 2 * TS), F32), sent],
        in_specs=[SMEM, SMEM, VMEM, VMEM],
        out_specs=[VMEM] * 3,
        compiler_params=params(8),
        name="split_terms",
    )(owners, offsets, mine, others)


STACK = pltpu.VMEM((POS, 2, 2 * TS + NP, TS), F32)


def fill(terms, stack):
    for p in range(POS):
        for part in range(2):
            cols = slice(part * TS, (part + 1) * TS)
            stack[p, part, :TS, :] = jnp.zeros((TS, TS), F32)
            stack[p, part, TS : TS + NP, :] = terms[p * NP : (p + 1) * NP, cols].astype(F32) * step_rate
            stack[p, part, TS + NP :, :] = jnp.zeros((TS, TS), F32)


def take_off(slots, rows, stack, tiles, done):
    for q in range(CAP):
        starts = []
        for p in range(POS):
            start = jnp.int32(0)
            for i in range(3):
                start = jnp.where(slots[p][i] == q, TS + i * TS - rows[p], start)
            starts.append(start)
        for part in range(2):
            tile = tiles[0, q, :, part * TS : (part + 1) * TS]
            for p in range(POS):
                tile = tile - stack[p, part, pl.ds(starts[p], TS), :]
            done(q, part, tile)


def keep(out):
    def done(q, part, tile):
        out[0, q, :, part * TS : (part + 1) * TS] = tile

    return done


def own_kernel(owners, offsets, tiles, terms, out, stack):
    slots = [[owners[0, p, 3 * i + 1] & (CAP - 1) for i in range(3)] for p in range(POS)]
    fill(terms, stack)
    take_off(slots, [offsets[0, p, 0] for p in range(POS)], stack, tiles, keep(out))


def own_update(owners, offsets, tiles, terms):
    return pl.pallas_call(
        own_kernel,
        out_shape=jax.ShapeDtypeStruct(tiles.shape, F32),
        in_specs=[SMEM, SMEM, VMEM, VMEM],
        out_specs=VMEM,
        scratch_shapes=[STACK],
        compiler_params=params(8),
        cost_estimate=pl.CostEstimate(flops=1_000_000, bytes_accessed=3_000_000, transcendentals=0),
        name="own_update",
    )(owners, offsets, tiles, terms)


def read_notes(j, terms, lines, notes, sem):
    lines[...] = terms[POS * NP :, :TS].astype(F32).astype(jnp.int32)
    copy = pltpu.make_async_copy(lines.at[0:1], notes, sem)
    copy.start()
    return copy


def noted(j, notes):
    slots = [[notes[0, p * 16 + 3 * i + j] for i in range(3)] for p in range(POS)]
    return slots, [notes[0, p * 16 + 9] for p in range(POS)]


NOTES = [STACK, pltpu.VMEM((16, TS), jnp.int32), pltpu.SMEM((1, TS), jnp.int32), pltpu.SemaphoreType.DMA(())]


def early_update_kernel(tiles, terms, out, stack, lines, notes, sem):
    j = 2 - 2 * early_side()
    copy = read_notes(j, terms, lines, notes, sem)
    fill(terms, stack)
    copy.wait()
    take_off(*noted(j, notes), stack, tiles, keep(out))


def early_update(tiles, terms):
    return pl.pallas_call(
        early_update_kernel,
        out_shape=jax.ShapeDtypeStruct(tiles.shape, F32),
        in_specs=[VMEM, VMEM],
        out_specs=VMEM,
        scratch_shapes=NOTES,
        compiler_params=params(8),
        cost_estimate=pl.CostEstimate(flops=1_000_000, bytes_accessed=3_000_000, transcendentals=0),
        name="early_update",
    )(tiles, terms)


def late_update_kernel(tiles, terms, out, stack, lines, notes, sem, work, sems):
    j = 2 * early_side()
    copy = read_notes(j, terms, lines, notes, sem)
    fill(terms, stack)
    copy.wait()
    copies = [pltpu.make_async_copy(work.at[0, q], out.at[0, q], sems.at[q]) for q in range(CAP)]

    def done(q, part, tile):
        keep(work)(q, part, tile)
        if part == 1:
            copies[q].start()

    take_off(*noted(j, notes), stack, tiles, done)
    for copy in copies:
        copy.wait()


def late_update(tiles, terms):
    return pl.pallas_call(
        late_update_kernel,
        out_shape=jax.ShapeDtypeStruct(tiles.shape, F32),
        in_specs=[VMEM, VMEM],
        out_specs=HBM,
        scratch_shapes=NOTES + [pltpu.VMEM((1, CAP, TS, 2 * TS), F32), pltpu.SemaphoreType.DMA((CAP,))],
        compiler_params=params(8),
        name="late_update",
    )(tiles, terms)


def swap(value, members, period):
    count = lax.axis_size("scan")
    pairs = [(i, (i + 1) % count) for i in range(count) if i % period in members]
    return lax.ppermute(value, "scan", pairs + [(j, i) for i, j in pairs])


def across(value):
    return lax.ppermute(value, "slab", [(0, 1), (1, 0)])


def shards(probe_modes, tap_weights, object_slices, exit_residual, offsets, owners):
    side = lax.axis_index("slab").astype(jnp.int32).reshape(1)
    own = object_slices[0].astype(BF16)
    first, second, third = swap(own, FIRST, 8), swap(own, SECOND, 8), swap(own, THIRD, 8)
    *mats, wave = exit_adjoint(side, tap_weights, exit_residual)
    partly = early_windows(owners, offsets, object_slices, first)
    t_there, t_near = late_windows(owners, offsets, second, third, partly)
    t_here = across(t_there)
    terms_there = slice_terms(False, t_near, probe_modes, wave, mats)
    terms_far = across(terms_there)
    terms_here = slice_terms(True, t_here, probe_modes, wave, mats)
    early_out, kept, late_out = split_terms(owners, offsets, terms_here, terms_far)
    late_in = swap(late_out, (1,), 2)
    early_in = swap(early_out, (0,), 2)
    tiles = own_update(owners, offsets, object_slices, kept)
    tiles = early_update(tiles, early_in)
    return late_update(tiles, late_in)


def solution(mesh):
    placed = (
        P(),
        P(),
        P("slab", "scan", None, None),
        P("scan", None, None, None, None),
        P("scan", None, None),
        P("scan", None, None),
    )
    return jax.shard_map(
        shards, mesh=mesh, in_specs=placed, out_specs=P("slab", "scan", None, None), check_vma=False
    )
```

```python
import functools

import jax
import jax.numpy as jnp
from jax import lax
from jax.experimental import pallas as pl
from jax.experimental.pallas import tpu as pltpu
from jax.sharding import PartitionSpec as P

step_rate = 0.125
F32, BF16 = jnp.float32, jnp.bfloat16
NP, TS, HALF = 256, 128, 15
MODES, POS, CAP = 4, 2, 8
STEP = 32
SMEM = pl.BlockSpec(memory_space=pltpu.SMEM)
VMEM = pl.BlockSpec(memory_space=pltpu.VMEM)
HBM = pl.BlockSpec(memory_space=pltpu.HBM)


def params(mib):
    return pltpu.CompilerParams(vmem_limit_bytes=mib * 1024 * 1024)


def dot(left, right):
    return jnp.dot(left, right, preferred_element_type=F32)


def lanes(rows):
    return lax.broadcasted_iota(jnp.int32, (rows, TS), 1)


def band(taps, row):
    wide = jnp.broadcast_to(taps[row : row + 1, :], (NP, NP))
    turned = pltpu.roll(wide, NP - HALF, 1, stride=1, stride_axis=0)
    gap = lax.broadcasted_iota(jnp.int32, (NP, NP), 1) - lax.broadcasted_iota(jnp.int32, (NP, NP), 0)
    return jnp.where(jnp.abs(gap) <= HALF, turned, 0.0)


def exit_kernel(taps, residual, left, left_adj, right, right_adj, wave, line):
    line[...] = jnp.zeros_like(line)
    for row in range(4):
        line[row : row + 1, 0 : 2 * HALF + 1] = taps[row // 2, row % 2 : row % 2 + 1, :].astype(F32)
    values = line[...]
    for first, plain, adj in ((0, left, left_adj), (2, right_adj, right)):
        re, im = band(values, first), band(values, first + 1)
        ret, imt = re.T, im.T
        plain[0:NP, 0:NP] = re.astype(BF16)
        plain[0:NP, NP:] = (-im).astype(BF16)
        plain[NP:, 0:NP] = im.astype(BF16)
        plain[NP:, NP:] = re.astype(BF16)
        adj[0:NP, 0:NP] = ret.astype(BF16)
        adj[0:NP, NP:] = imt.astype(BF16)
        adj[NP:, 0:NP] = (-imt).astype(BF16)
        adj[NP:, NP:] = ret.astype(BF16)
    for m in range(MODES):
        w = dot(residual[0, 0, m], right_adj[...]).astype(BF16)
        w = jnp.concatenate([w[:, :NP], w[:, NP:]], 0)
        wave[m] = dot(left_adj[...], w).astype(BF16)


def exit_adjoint(side, taps, residual):
    whole = lambda *shape: pl.BlockSpec(shape, lambda i, side: (0,) * len(shape))
    return pl.pallas_call(
        lambda side, *refs: exit_kernel(*refs),
        grid_spec=pltpu.PrefetchScalarGridSpec(
            num_scalar_prefetch=1,
            grid=(1,),
            in_specs=[
                whole(2, 2, 2 * HALF + 1),
                pl.BlockSpec((1, 1, MODES, NP, 2 * NP), lambda i, side: (0, side[0], 0, 0, 0)),
            ],
            out_specs=[whole(2 * NP, 2 * NP)] * 4 + [whole(MODES, 2 * NP, NP)],
            scratch_shapes=[pltpu.VMEM((8, NP), F32)],
        ),
        out_shape=[jax.ShapeDtypeStruct((2 * NP, 2 * NP), BF16)] * 4
        + [jax.ShapeDtypeStruct((MODES, 2 * NP, NP), BF16)],
        compiler_params=params(24),
        cost_estimate=pl.CostEstimate(flops=1_100_000_000, bytes_accessed=6_000_000, transcendentals=0),
        name="exit_adjoint",
    )(side, taps, residual)


FIRST, SECOND, THIRD = (0, 2, 4), (5, 7), (1, 3, 6)


def part_in(members):
    z = lax.axis_index("scan") % 8
    right = functools.reduce(jnp.logical_or, [z == i for i in members])
    left = functools.reduce(jnp.logical_or, [z == (i + 1) % 8 for i in members])
    return jnp.logical_or(left, right), right.astype(jnp.int32)


def early_side():
    return 1 - lax.axis_index("scan") % 2


def packed_tile(tiles):
    return lambda q: tiles[q].astype(F32)


def plain_tile(tiles):
    return lambda q: tiles[0, q].astype(BF16).astype(F32)


def cut_column(p, j, owners, offsets, tile_at, stack, put):
    for i in range(3):
        tile = tile_at(owners[0, p, 3 * i + j] & (CAP - 1))
        stack[0, i * TS : (i + 1) * TS, :] = tile[:, :TS]
        stack[1, i * TS : (i + 1) * TS, :] = tile[:, TS:]
    r, c = offsets[0, p, 0], offsets[0, p, 1]
    back = (TS - c) & (TS - 1)
    for at in range(0, NP, STEP):
        for part in range(2):
            put(part, at, pltpu.roll(stack[part, pl.ds(r + at, STEP), :], back, 1))


def half(side):
    return pl.ds(pl.multiple_of(side * TS, TS), TS)


def taken(side, c):
    past = lanes(STEP) - (TS - c)
    return past * (1 - 2 * side) - side < 0


def early_kernel(owners, offsets, own, first, out, stack):
    inside, side = part_in(FIRST)
    for p in range(POS):

        def put_own(part, at, turned):
            out[p, part, at : at + STEP, :TS] = turned
            out[p, part, at : at + STEP, TS:] = turned

        cut_column(p, 1, owners, offsets, plain_tile(own), stack.at[0], put_own)

    @pl.when(inside)
    def _():
        for p in range(POS):
            overlay(p, side, owners, offsets, first, stack.at[1], out.at[p], out.at[p])


def overlay(p, side, owners, offsets, tiles, stack, base, out):
    mask = taken(side, offsets[0, p, 1])

    def put(part, at, turned):
        place = (part, slice(at, at + STEP), half(side))
        out[place] = jnp.where(mask, turned, base[place]).astype(out.dtype)

    cut_column(p, 2 * side, owners, offsets, packed_tile(tiles), stack, put)


def early_windows(owners, offsets, own, first):
    return pl.pallas_call(
        early_kernel,
        out_shape=jax.ShapeDtypeStruct((POS, 2, NP, NP), F32),
        in_specs=[SMEM, SMEM, VMEM, VMEM],
        out_specs=VMEM,
        scratch_shapes=[pltpu.VMEM((2, 2, 3 * TS, TS), F32)],
        compiler_params=params(8),
        cost_estimate=pl.CostEstimate(flops=2_000_000, bytes_accessed=2_000_000, transcendentals=0),
        name="early_windows",
    )(owners, offsets, own, first)


def late_kernel(owners, offsets, third, second, partly, far, near, stack):
    here = lax.axis_index("slab")
    far[...] = partly[1 - here].astype(BF16)
    near[...] = partly[here].astype(BF16)
    for k, (members, tiles) in enumerate(((SECOND, second), (THIRD, third))):
        inside, side = part_in(members)

        @pl.when(inside)
        def _():
            for n, (p, out) in enumerate(((1 - here, far), (here, near))):
                overlay(p, side, owners, offsets, tiles, stack.at[2 * k + n], partly.at[p], out)


def late_windows(owners, offsets, second, third, partly):
    return pl.pallas_call(
        late_kernel,
        out_shape=[jax.ShapeDtypeStruct((2, NP, NP), BF16)] * 2,
        in_specs=[SMEM, SMEM, VMEM, VMEM, VMEM],
        out_specs=[VMEM] * 2,
        scratch_shapes=[pltpu.VMEM((4, 2, 3 * TS, TS), F32)],
        compiler_params=params(8),
        cost_estimate=pl.CostEstimate(flops=1_000_000, bytes_accessed=2_000_000, transcendentals=0),
        name="late_windows",
    )(owners, offsets, third, second, partly)


def times(a, b, conjugate):
    (ar, ai), (br, bi) = a, b
    if conjugate:
        return ar * br + ai * bi, ar * bi - ai * br
    return ar * br - ai * bi, ar * bi + ai * br


def beside(ref, m):
    return ref[m, :, :NP].astype(F32), ref[m, :, NP:].astype(F32)


def above(ref, m):
    return ref[m, :NP, :].astype(F32), ref[m, NP:, :].astype(F32)


def summed(pairs, total):
    for at in range(0, NP, STEP):
        rows = slice(at, at + STEP)
        re = im = None
        for left, right in pairs(rows):
            one_re, one_im = times(left, right, True)
            re, im = (one_re, one_im) if re is None else (re + one_re, im + one_im)
        total[0, rows, :], total[1, rows, :] = re.astype(total.dtype), im.astype(total.dtype)


def wide(ref, m, rows):
    return ref[m, rows, :NP].astype(F32), ref[m, rows, NP:].astype(F32)


def tall(ref, m, rows):
    return ref[m, rows, :].astype(F32), ref[m, slice(NP + rows.start, NP + rows.stop), :].astype(F32)


def lower_terms(t, probe, wave, left, right, total, rows_in, waves):
    window = (t[0].astype(F32), t[1].astype(F32))
    for m in range(MODES):
        u = jnp.concatenate(times(beside(probe, m), window, False), 0).astype(BF16)
        v = dot(left[...], u).astype(BF16)
        rows_in[m * NP : (m + 1) * NP, :NP] = v[:NP]
        rows_in[m * NP : (m + 1) * NP, NP:] = v[NP:]
    waves[...] = dot(rows_in[...], right[...]).reshape(MODES, NP, 2 * NP)
    summed(lambda rows: [(wide(waves, m, rows), tall(wave, m, rows)) for m in range(MODES)], total)


def upper_terms(t, probe, wave, left_adj, right_adj, total, rows_in, waves):
    window = (t[0].astype(F32), t[1].astype(F32))
    for m in range(MODES):
        re, im = times(window, above(wave, m), True)
        rows_in[m * NP : (m + 1) * NP, :NP] = re.astype(BF16)
        rows_in[m * NP : (m + 1) * NP, NP:] = im.astype(BF16)
    w = dot(rows_in[...], right_adj[...]).astype(BF16)
    for m in range(MODES):
        part = w[m * NP : (m + 1) * NP]
        waves[m] = dot(left_adj[...], jnp.concatenate([part[:, :NP], part[:, NP:]], 0))
    summed(lambda rows: [(wide(probe, m, rows), tall(waves, m, rows)) for m in range(MODES)], total)


def terms_kernel(far, t, probe, wave, left, left_adj, right, right_adj, out, rows_in, lower, upper):
    side = lax.axis_index("slab")
    chosen = 1 - side if far else side

    @pl.when(chosen == 0)
    def _():
        lower_terms(t, probe, wave, left, right, out, rows_in, lower)

    @pl.when(chosen == 1)
    def _():
        upper_terms(t, probe, wave, left_adj, right_adj, out, rows_in, upper)


def slice_terms(far, t, probe, wave, mats):
    return pl.pallas_call(
        functools.partial(terms_kernel, far),
        out_shape=jax.ShapeDtypeStruct((2, NP, NP), F32 if far else BF16),
        in_specs=[VMEM] * 7,
        out_specs=VMEM,
        scratch_shapes=[
            pltpu.VMEM((MODES * NP, 2 * NP), BF16),
            pltpu.VMEM((MODES, NP, 2 * NP), F32),
            pltpu.VMEM((MODES, 2 * NP, NP), F32),
        ],
        compiler_params=params(32),
        cost_estimate=pl.CostEstimate(flops=1_100_000_000, bytes_accessed=5_000_000, transcendentals=0),
        name="far_terms" if far else "near_terms",
    )(t, probe, wave, *mats)


def split_kernel(owners, offsets, mine, others, early, late):
    here = lax.axis_index("slab")
    place = lax.broadcasted_iota(jnp.int32, (16, 2 * TS), 1)
    notes = jnp.zeros((16, 2 * TS), jnp.int32)
    for p in range(POS):
        for k in range(9):
            notes = jnp.where(place == p * 16 + k, owners[0, p, k] & (CAP - 1), notes)
        notes = jnp.where(place == p * 16 + 9, offsets[0, p, 0], notes)
    early[POS * NP :, :] = notes.astype(F32).astype(BF16)
    late[POS * NP :, :] = notes.astype(F32).astype(BF16)
    to_right = early_side() == 1
    spot = lanes(STEP)
    for k, terms in ((0, mine), (1, others)):
        p = here if k == 0 else 1 - here
        c = offsets[0, p, 1]
        for at in range(0, NP, STEP):
            for part in range(2):
                low = pltpu.roll(terms[part, at : at + STEP, 0:TS].astype(F32), c, 1)
                high = pltpu.roll(terms[part, at : at + STEP, TS:].astype(F32), c, 1)
                place = (pl.ds(p * NP + at, STEP), slice(part * TS, (part + 1) * TS))
                left = jnp.where(spot >= c, low, 0.0)
                right = jnp.where(spot < c, high, 0.0)
                early[place] = jnp.where(to_right, right, left).astype(BF16)
                late[place] = jnp.where(to_right, left, right).astype(BF16)


def split_terms(owners, offsets, mine, others):
    sent = jax.ShapeDtypeStruct((POS * NP + 16, 2 * TS), BF16)
    return pl.pallas_call(
        split_kernel,
        out_shape=[sent, sent],
        in_specs=[SMEM, SMEM, VMEM, VMEM],
        out_specs=[VMEM] * 2,
        compiler_params=params(8),
        name="split_terms",
    )(owners, offsets, mine, others)


STACK = pltpu.VMEM((POS, 2, 2 * TS + NP, TS), F32)


def clear(stack):
    for p in range(POS):
        for part in range(2):
            stack[p, part, :TS, :] = jnp.zeros((TS, TS), F32)
            stack[p, part, TS + NP :, :] = jnp.zeros((TS, TS), F32)


def fill(terms, stack):
    clear(stack)
    for p in range(POS):
        for part in range(2):
            cols = slice(part * TS, (part + 1) * TS)
            stack[p, part, TS : TS + NP, :] = terms[p * NP : (p + 1) * NP, cols].astype(F32) * step_rate


def take_off(slots, rows, stack, tiles, done):
    for q in range(CAP):
        starts = []
        for p in range(POS):
            start = jnp.int32(0)
            for i in range(3):
                start = jnp.where(slots[p][i] == q, TS + i * TS - rows[p], start)
            starts.append(start)
        for part in range(2):
            tile = tiles[0, q, :, part * TS : (part + 1) * TS]
            for p in range(POS):
                tile = tile - stack[p, part, pl.ds(starts[p], TS), :]
            done(q, part, tile)


def keep(out):
    def done(q, part, tile):
        out[0, q, :, part * TS : (part + 1) * TS] = tile

    return done


def own_kernel(owners, offsets, tiles, mine, others, out, stack):
    here = lax.axis_index("slab")
    spot = lanes(STEP)
    clear(stack)
    for k, terms in ((0, mine), (1, others)):
        p = here if k == 0 else 1 - here
        c = offsets[0, p, 1]
        for at in range(0, NP, STEP):
            for part in range(2):
                low = pltpu.roll(terms[part, at : at + STEP, 0:TS].astype(F32), c, 1)
                high = pltpu.roll(terms[part, at : at + STEP, TS:].astype(F32), c, 1)
                stack[p, part, TS + at : TS + at + STEP, :] = jnp.where(spot < c, low, high) * step_rate
    slots = [[owners[0, p, 3 * i + 1] & (CAP - 1) for i in range(3)] for p in range(POS)]
    take_off(slots, [offsets[0, p, 0] for p in range(POS)], stack, tiles, keep(out))


def own_update(owners, offsets, tiles, mine, others):
    return pl.pallas_call(
        own_kernel,
        out_shape=jax.ShapeDtypeStruct(tiles.shape, F32),
        in_specs=[SMEM, SMEM, VMEM, VMEM, VMEM],
        out_specs=VMEM,
        scratch_shapes=[STACK],
        compiler_params=params(8),
        cost_estimate=pl.CostEstimate(flops=1_000_000, bytes_accessed=3_000_000, transcendentals=0),
        name="own_update",
    )(owners, offsets, tiles, mine, others)


def read_notes(j, terms, lines, notes, sem):
    lines[...] = terms[POS * NP :, :TS].astype(F32).astype(jnp.int32)
    copy = pltpu.make_async_copy(lines.at[0:1], notes, sem)
    copy.start()
    return copy


def noted(j, notes):
    slots = [[notes[0, p * 16 + 3 * i + j] for i in range(3)] for p in range(POS)]
    return slots, [notes[0, p * 16 + 9] for p in range(POS)]


NOTES = [STACK, pltpu.VMEM((16, TS), jnp.int32), pltpu.SMEM((1, TS), jnp.int32), pltpu.SemaphoreType.DMA(())]


def early_update_kernel(tiles, terms, out, stack, lines, notes, sem):
    j = 2 - 2 * early_side()
    copy = read_notes(j, terms, lines, notes, sem)
    fill(terms, stack)
    copy.wait()
    take_off(*noted(j, notes), stack, tiles, keep(out))


def early_update(tiles, terms):
    return pl.pallas_call(
        early_update_kernel,
        out_shape=jax.ShapeDtypeStruct(tiles.shape, F32),
        in_specs=[VMEM, VMEM],
        out_specs=VMEM,
        scratch_shapes=NOTES,
        compiler_params=params(8),
        cost_estimate=pl.CostEstimate(flops=1_000_000, bytes_accessed=3_000_000, transcendentals=0),
        name="early_update",
    )(tiles, terms)


def late_update_kernel(tiles, terms, out, stack, lines, notes, sem, work, sems):
    j = 2 * early_side()
    copy = read_notes(j, terms, lines, notes, sem)
    fill(terms, stack)
    copy.wait()
    copies = [pltpu.make_async_copy(work.at[0, q], out.at[0, q], sems.at[q]) for q in range(CAP)]

    def done(q, part, tile):
        keep(work)(q, part, tile)
        if part == 1:
            copies[q].start()

    take_off(*noted(j, notes), stack, tiles, done)
    for copy in copies:
        copy.wait()


def late_update(tiles, terms):
    return pl.pallas_call(
        late_update_kernel,
        out_shape=jax.ShapeDtypeStruct(tiles.shape, F32),
        in_specs=[VMEM, VMEM],
        out_specs=HBM,
        scratch_shapes=NOTES + [pltpu.VMEM((1, CAP, TS, 2 * TS), F32), pltpu.SemaphoreType.DMA((CAP,))],
        compiler_params=params(8),
        name="late_update",
    )(tiles, terms)


def swap(value, members, period):
    count = lax.axis_size("scan")
    pairs = [(i, (i + 1) % count) for i in range(count) if i % period in members]
    pairs += [(j, i) for i, j in pairs]
    inside = {i for i, _ in pairs}
    return lax.ppermute(value, "scan", pairs + [(i, i) for i in range(count) if i not in inside])


def across(value):
    return lax.ppermute(value, "slab", [(0, 1), (1, 0)])


def shards(probe_modes, tap_weights, object_slices, exit_residual, offsets, owners):
    side = lax.axis_index("slab").astype(jnp.int32).reshape(1)
    own = object_slices[0].astype(BF16)
    first, second, third = swap(own, FIRST, 8), swap(own, SECOND, 8), swap(own, THIRD, 8)
    *mats, wave = exit_adjoint(side, tap_weights, exit_residual)
    partly = early_windows(owners, offsets, object_slices, first)
    t_there, t_near = late_windows(owners, offsets, second, third, partly)
    t_here = across(t_there)
    terms_there = slice_terms(False, t_near, probe_modes, wave, mats)
    terms_far = across(terms_there)
    terms_here = slice_terms(True, t_here, probe_modes, wave, mats)
    early_out, late_out = split_terms(owners, offsets, terms_here, terms_far)
    late_in = swap(late_out, (1,), 2)
    early_in = swap(early_out, (0,), 2)
    tiles = own_update(owners, offsets, object_slices, terms_here, terms_far)
    tiles = early_update(tiles, early_in)
    return late_update(tiles, late_in)


def solution(mesh):
    placed = (
        P(),
        P(),
        P("slab", "scan", None, None),
        P("scan", None, None, None, None),
        P("scan", None, None),
        P("scan", None, None),
    )
    return jax.shard_map(
        shards, mesh=mesh, in_specs=placed, out_specs=P("slab", "scan", None, None), check_vma=False
    )
```

```python
import functools

import jax
import jax.numpy as jnp
from jax import lax
from jax.experimental import pallas as pl
from jax.experimental.pallas import tpu as pltpu
from jax.sharding import PartitionSpec as P

step_rate = 0.125
F32, BF16 = jnp.float32, jnp.bfloat16
NP, TS, HALF = 256, 128, 15
MODES, POS, CAP = 4, 2, 8
STEP = 32
VMEM = pl.BlockSpec(memory_space=pltpu.VMEM)
HBM = pl.BlockSpec(memory_space=pltpu.HBM)


def params(mib):
    return pltpu.CompilerParams(vmem_limit_bytes=mib * 1024 * 1024)


def dot(left, right):
    return jnp.dot(left, right, preferred_element_type=F32)


class Table:
    def __init__(self, values):
        self.values = values.astype(F32)
        self.row, self.lane = (lax.broadcasted_iota(jnp.int32, values.shape, axis) for axis in range(2))

    def at(self, row, lane):
        return jnp.sum(jnp.where((self.row == row) & (self.lane == lane), self.values, 0.0)).astype(jnp.int32)


def lanes(rows):
    return lax.broadcasted_iota(jnp.int32, (rows, TS), 1)


def band(taps, row):
    wide = jnp.broadcast_to(taps[row : row + 1, :], (NP, NP))
    turned = pltpu.roll(wide, NP - HALF, 1, stride=1, stride_axis=0)
    gap = lax.broadcasted_iota(jnp.int32, (NP, NP), 1) - lax.broadcasted_iota(jnp.int32, (NP, NP), 0)
    return jnp.where(jnp.abs(gap) <= HALF, turned, 0.0)


def exit_kernel(taps, residual, left, left_adj, right, right_adj, wave, line):
    line[...] = jnp.zeros_like(line)
    for row in range(4):
        line[row : row + 1, 0 : 2 * HALF + 1] = taps[row // 2, row % 2 : row % 2 + 1, :].astype(F32)
    values = line[...]
    for first, plain, adj in ((0, left, left_adj), (2, right_adj, right)):
        re, im = band(values, first), band(values, first + 1)
        ret, imt = re.T, im.T
        plain[0:NP, 0:NP] = re.astype(BF16)
        plain[0:NP, NP:] = (-im).astype(BF16)
        plain[NP:, 0:NP] = im.astype(BF16)
        plain[NP:, NP:] = re.astype(BF16)
        adj[0:NP, 0:NP] = ret.astype(BF16)
        adj[0:NP, NP:] = imt.astype(BF16)
        adj[NP:, 0:NP] = (-imt).astype(BF16)
        adj[NP:, NP:] = ret.astype(BF16)
    for m in range(MODES):
        w = dot(residual[0, 0, m], right_adj[...]).astype(BF16)
        w = jnp.concatenate([w[:, :NP], w[:, NP:]], 0)
        wave[m] = dot(left_adj[...], w).astype(BF16)


def exit_adjoint(side, taps, residual):
    whole = lambda *shape: pl.BlockSpec(shape, lambda i, side: (0,) * len(shape))
    return pl.pallas_call(
        lambda side, *refs: exit_kernel(*refs),
        grid_spec=pltpu.PrefetchScalarGridSpec(
            num_scalar_prefetch=1,
            grid=(1,),
            in_specs=[
                whole(2, 2, 2 * HALF + 1),
                pl.BlockSpec((1, 1, MODES, NP, 2 * NP), lambda i, side: (0, side[0], 0, 0, 0)),
            ],
            out_specs=[whole(2 * NP, 2 * NP)] * 4 + [whole(MODES, 2 * NP, NP)],
            scratch_shapes=[pltpu.VMEM((8, NP), F32)],
        ),
        out_shape=[jax.ShapeDtypeStruct((2 * NP, 2 * NP), BF16)] * 4
        + [jax.ShapeDtypeStruct((MODES, 2 * NP, NP), BF16)],
        compiler_params=params(24),
        cost_estimate=pl.CostEstimate(flops=1_100_000_000, bytes_accessed=6_000_000, transcendentals=0),
        name="exit_adjoint",
    )(side, taps, residual)


def early_side():
    return 1 - lax.axis_index("scan") % 2


def packed_tile(tiles):
    return lambda q: tiles[q].astype(F32)


def plain_tile(tiles):
    return lambda q: tiles[0, q].astype(BF16).astype(F32)


def cut_column(p, j, owners, offsets, tile_at, stack, put):
    for i in range(3):
        tile = tile_at(owners.at(p, 3 * i + j) & (CAP - 1))
        stack[0, i * TS : (i + 1) * TS, :] = tile[:, :TS]
        stack[1, i * TS : (i + 1) * TS, :] = tile[:, TS:]
    r, c = offsets.at(p, 0), offsets.at(p, 1)
    back = (TS - c) & (TS - 1)
    for at in range(0, NP, STEP):
        for part in range(2):
            put(part, at, pltpu.roll(stack[part, pl.ds(r + at, STEP), :], back, 1))


def half(side):
    return pl.ds(pl.multiple_of(side * TS, TS), TS)


def taken(side, c):
    past = lanes(STEP) - (TS - c)
    return past * (1 - 2 * side) - side < 0


def early_kernel(owners, offsets, own, early, out, stack):
    owners, offsets = Table(owners[0]), Table(offsets[0])
    side = early_side()
    for p in range(POS):

        def put_own(part, at, turned):
            out[p, part, at : at + STEP, :TS] = turned
            out[p, part, at : at + STEP, TS:] = turned

        cut_column(p, 1, owners, offsets, plain_tile(own), stack.at[0], put_own)
        mask = taken(side, offsets.at(p, 1))

        def put_early(part, at, turned):
            place = (p, part, slice(at, at + STEP), half(side))
            out[place] = jnp.where(mask, turned, out[place])

        cut_column(p, 2 * side, owners, offsets, packed_tile(early), stack.at[1], put_early)


def early_windows(owners, offsets, own, early):
    return pl.pallas_call(
        early_kernel,
        out_shape=jax.ShapeDtypeStruct((POS, 2, NP, NP), F32),
        in_specs=[VMEM] * 4,
        out_specs=VMEM,
        scratch_shapes=[pltpu.VMEM((2, 2, 3 * TS, TS), F32)],
        compiler_params=params(8),
        cost_estimate=pl.CostEstimate(flops=2_000_000, bytes_accessed=2_000_000, transcendentals=0),
        name="early_windows",
    )(owners, offsets, own, early)


def complete(p, owners, offsets, late, partly, stack, out):
    side = 1 - early_side()
    mask = taken(side, offsets.at(p, 1))

    def put(part, at, turned):
        rows = slice(at, at + STEP)
        kept = partly[p, part, rows, half(side)]
        out[part, rows, half(side)] = jnp.where(mask, turned, kept).astype(out.dtype)
        out[part, rows, half(1 - side)] = partly[p, part, rows, half(1 - side)].astype(out.dtype)

    cut_column(p, 2 * side, owners, offsets, packed_tile(late), stack, put)


def late_kernel(owners, offsets, late, partly, far, near, stack):
    owners, offsets = Table(owners[0]), Table(offsets[0])
    here = lax.axis_index("slab")
    complete(1 - here, owners, offsets, late, partly, stack.at[0], far)
    complete(here, owners, offsets, late, partly, stack.at[1], near)


def late_windows(owners, offsets, late, partly):
    return pl.pallas_call(
        late_kernel,
        out_shape=[jax.ShapeDtypeStruct((2, NP, NP), BF16)] * 2,
        in_specs=[VMEM] * 4,
        out_specs=[VMEM] * 2,
        scratch_shapes=[pltpu.VMEM((2, 2, 3 * TS, TS), F32)],
        compiler_params=params(8),
        cost_estimate=pl.CostEstimate(flops=1_000_000, bytes_accessed=2_000_000, transcendentals=0),
        name="late_windows",
    )(owners, offsets, late, partly)


def times(a, b, conjugate):
    (ar, ai), (br, bi) = a, b
    if conjugate:
        return ar * br + ai * bi, ar * bi - ai * br
    return ar * br - ai * bi, ar * bi + ai * br


def beside(ref, m):
    return ref[m, :, :NP].astype(F32), ref[m, :, NP:].astype(F32)


def above(ref, m):
    return ref[m, :NP, :].astype(F32), ref[m, NP:, :].astype(F32)


def summed(pairs, total):
    for at in range(0, NP, STEP):
        rows = slice(at, at + STEP)
        re = im = None
        for left, right in pairs(rows):
            one_re, one_im = times(left, right, True)
            re, im = (one_re, one_im) if re is None else (re + one_re, im + one_im)
        total[0, rows, :], total[1, rows, :] = re.astype(total.dtype), im.astype(total.dtype)


def wide(ref, m, rows):
    return ref[m, rows, :NP].astype(F32), ref[m, rows, NP:].astype(F32)


def tall(ref, m, rows):
    return ref[m, rows, :].astype(F32), ref[m, slice(NP + rows.start, NP + rows.stop), :].astype(F32)


def lower_terms(t, probe, wave, left, right, total, rows_in, waves):
    window = (t[0].astype(F32), t[1].astype(F32))
    for m in range(MODES):
        u = jnp.concatenate(times(beside(probe, m), window, False), 0).astype(BF16)
        v = dot(left[...], u).astype(BF16)
        rows_in[m * NP : (m + 1) * NP, :NP] = v[:NP]
        rows_in[m * NP : (m + 1) * NP, NP:] = v[NP:]
    waves[...] = dot(rows_in[...], right[...]).reshape(MODES, NP, 2 * NP)
    summed(lambda rows: [(wide(waves, m, rows), tall(wave, m, rows)) for m in range(MODES)], total)


def upper_terms(t, probe, wave, left_adj, right_adj, total, rows_in, waves):
    window = (t[0].astype(F32), t[1].astype(F32))
    for m in range(MODES):
        re, im = times(window, above(wave, m), True)
        rows_in[m * NP : (m + 1) * NP, :NP] = re.astype(BF16)
        rows_in[m * NP : (m + 1) * NP, NP:] = im.astype(BF16)
    w = dot(rows_in[...], right_adj[...]).astype(BF16)
    for m in range(MODES):
        part = w[m * NP : (m + 1) * NP]
        waves[m] = dot(left_adj[...], jnp.concatenate([part[:, :NP], part[:, NP:]], 0))
    summed(lambda rows: [(wide(probe, m, rows), tall(waves, m, rows)) for m in range(MODES)], total)


def terms_kernel(far, t, probe, wave, left, left_adj, right, right_adj, out, rows_in, lower, upper):
    side = lax.axis_index("slab")
    chosen = 1 - side if far else side

    @pl.when(chosen == 0)
    def _():
        lower_terms(t, probe, wave, left, right, out, rows_in, lower)

    @pl.when(chosen == 1)
    def _():
        upper_terms(t, probe, wave, left_adj, right_adj, out, rows_in, upper)


def slice_terms(far, t, probe, wave, mats):
    return pl.pallas_call(
        functools.partial(terms_kernel, far),
        out_shape=jax.ShapeDtypeStruct((2, NP, NP), F32 if far else BF16),
        in_specs=[VMEM] * 7,
        out_specs=VMEM,
        scratch_shapes=[
            pltpu.VMEM((MODES * NP, 2 * NP), BF16),
            pltpu.VMEM((MODES, NP, 2 * NP), F32),
            pltpu.VMEM((MODES, 2 * NP, NP), F32),
        ],
        compiler_params=params(32),
        cost_estimate=pl.CostEstimate(flops=1_100_000_000, bytes_accessed=5_000_000, transcendentals=0),
        name="far_terms" if far else "near_terms",
    )(t, probe, wave, *mats)


def split_kernel(owners, offsets, mine, others, early, late, notes):
    here = lax.axis_index("slab")
    notes[...] = jnp.zeros_like(notes)
    notes[0:POS, 0:9] = (owners[0] & (CAP - 1)).astype(F32)
    notes[POS : 2 * POS, 0:2] = offsets[0].astype(F32)
    early[POS * NP :, :] = notes[...].astype(BF16)
    late[POS * NP :, :] = notes[...].astype(BF16)
    offsets = Table(offsets[0])
    to_right = early_side() == 1
    spot = lanes(STEP)
    for k, terms in ((0, mine), (1, others)):
        p = here if k == 0 else 1 - here
        c = offsets.at(p, 1)
        for at in range(0, NP, STEP):
            for part in range(2):
                low = pltpu.roll(terms[part, at : at + STEP, 0:TS].astype(F32), c, 1)
                high = pltpu.roll(terms[part, at : at + STEP, TS:].astype(F32), c, 1)
                place = (pl.ds(p * NP + at, STEP), slice(part * TS, (part + 1) * TS))
                left = jnp.where(spot >= c, low, 0.0)
                right = jnp.where(spot < c, high, 0.0)
                early[place] = jnp.where(to_right, right, left).astype(BF16)
                late[place] = jnp.where(to_right, left, right).astype(BF16)


def split_terms(owners, offsets, mine, others):
    sent = jax.ShapeDtypeStruct((POS * NP + 16, 2 * TS), BF16)
    return pl.pallas_call(
        split_kernel,
        out_shape=[sent, sent],
        in_specs=[VMEM] * 4,
        out_specs=[VMEM] * 2,
        scratch_shapes=[pltpu.VMEM((16, 2 * TS), F32)],
        compiler_params=params(8),
        name="split_terms",
    )(owners, offsets, mine, others)


STACK = pltpu.VMEM((POS, 2, 2 * TS + NP, TS), F32)


def clear(stack):
    for p in range(POS):
        for part in range(2):
            stack[p, part, :TS, :] = jnp.zeros((TS, TS), F32)
            stack[p, part, TS + NP :, :] = jnp.zeros((TS, TS), F32)


def fill(terms, stack):
    clear(stack)
    for p in range(POS):
        for part in range(2):
            cols = slice(part * TS, (part + 1) * TS)
            stack[p, part, TS : TS + NP, :] = terms[p * NP : (p + 1) * NP, cols].astype(F32) * step_rate


def take_off(q, slots, rows, stack, tiles, out):
    starts = []
    for p in range(POS):
        start = jnp.int32(0)
        for i in range(3):
            start = jnp.where(slots[p][i] == q, TS + i * TS - rows[p], start)
        starts.append(start)
    for part in range(2):
        cols = slice(part * TS, (part + 1) * TS)
        tile = tiles[0, q, :, cols]
        for p in range(POS):
            tile = tile - stack[p, part, pl.ds(starts[p], TS), :]
        out[0, q, :, cols] = tile


def own_kernel(owners, offsets, tiles, mine, others, out, stack):
    owners, offsets = Table(owners[0]), Table(offsets[0])
    here = lax.axis_index("slab")
    spot = lanes(STEP)
    clear(stack)
    for k, terms in ((0, mine), (1, others)):
        p = here if k == 0 else 1 - here
        c = offsets.at(p, 1)
        for at in range(0, NP, STEP):
            for part in range(2):
                low = pltpu.roll(terms[part, at : at + STEP, 0:TS].astype(F32), c, 1)
                high = pltpu.roll(terms[part, at : at + STEP, TS:].astype(F32), c, 1)
                stack[p, part, TS + at : TS + at + STEP, :] = jnp.where(spot < c, low, high) * step_rate
    slots = [[owners.at(p, 3 * i + 1) & (CAP - 1) for i in range(3)] for p in range(POS)]
    for q in range(CAP):
        take_off(q, slots, [offsets.at(p, 0) for p in range(POS)], stack, tiles, out)


def own_update(owners, offsets, tiles, mine, others):
    return pl.pallas_call(
        own_kernel,
        out_shape=jax.ShapeDtypeStruct(tiles.shape, F32),
        in_specs=[VMEM] * 5,
        out_specs=VMEM,
        scratch_shapes=[STACK],
        compiler_params=params(8),
        cost_estimate=pl.CostEstimate(flops=1_000_000, bytes_accessed=3_000_000, transcendentals=0),
        name="own_update",
    )(owners, offsets, tiles, mine, others)


def noted(j, terms):
    notes = Table(terms[POS * NP :, :TS])
    slots = [[notes.at(p, 3 * i + j) for i in range(3)] for p in range(POS)]
    return slots, [notes.at(POS + p, 0) for p in range(POS)]


def early_update_kernel(tiles, terms, out, whole, stack, sems):
    j = 2 - 2 * early_side()
    slots, rows = noted(j, terms)
    fill(terms, stack)
    for q in range(CAP):
        take_off(q, slots, rows, stack, tiles, out)
        pltpu.make_async_copy(out.at[0, q], whole.at[0, q], sems.at[q]).start()
    for q in range(CAP):
        pltpu.make_async_copy(out.at[0, q], whole.at[0, q], sems.at[q]).wait()


def early_update(tiles, terms):
    return pl.pallas_call(
        early_update_kernel,
        out_shape=[jax.ShapeDtypeStruct(tiles.shape, F32)] * 2,
        in_specs=[VMEM, VMEM],
        out_specs=[VMEM, HBM],
        scratch_shapes=[STACK, pltpu.SemaphoreType.DMA((CAP,))],
        compiler_params=params(8),
        cost_estimate=pl.CostEstimate(flops=1_000_000, bytes_accessed=3_000_000, transcendentals=0),
        name="early_update",
    )(tiles, terms)


def late_update_kernel(tiles, terms, whole, out, stack, work, sems):
    j = 2 * early_side()
    slots, rows = noted(j, terms)
    fill(terms, stack)
    touched = [
        functools.reduce(jnp.logical_or, [slots[p][i] == q for p in range(POS) for i in range(3)]) for q in range(CAP)
    ]
    for q in range(CAP):

        @pl.when(touched[q])
        def _():
            take_off(q, slots, rows, stack, tiles, work)
            pltpu.make_async_copy(work.at[0, q], out.at[0, q], sems.at[q]).start()

    for q in range(CAP):

        @pl.when(touched[q])
        def _():
            pltpu.make_async_copy(work.at[0, q], out.at[0, q], sems.at[q]).wait()


def late_update(tiles, terms, whole):
    return pl.pallas_call(
        late_update_kernel,
        out_shape=jax.ShapeDtypeStruct(tiles.shape, F32),
        in_specs=[VMEM, VMEM, HBM],
        out_specs=HBM,
        input_output_aliases={2: 0},
        scratch_shapes=[STACK, pltpu.VMEM((1, CAP, TS, 2 * TS), F32), pltpu.SemaphoreType.DMA((CAP,))],
        compiler_params=params(8),
        name="late_update",
    )(tiles, terms, whole)


def swap(value, first):
    count = lax.axis_size("scan")
    pairs = [(i, (i + 1) % count) for i in range(first, count, 2)]
    return lax.ppermute(value, "scan", pairs + [(j, i) for i, j in pairs])


def across(value):
    return lax.ppermute(value, "slab", [(0, 1), (1, 0)])


def shards(probe_modes, tap_weights, object_slices, exit_residual, offsets, owners):
    side = lax.axis_index("slab").astype(jnp.int32).reshape(1)
    own = object_slices[0].astype(BF16)
    late = swap(own, 1)
    early = swap(own, 0)
    *mats, wave = exit_adjoint(side, tap_weights, exit_residual)
    partly = early_windows(owners, offsets, object_slices, early)
    t_there, t_near = late_windows(owners, offsets, late, partly)
    t_here = across(t_there)
    terms_there = slice_terms(False, t_near, probe_modes, wave, mats)
    terms_far = across(terms_there)
    terms_here = slice_terms(True, t_here, probe_modes, wave, mats)
    early_out, late_out = split_terms(owners, offsets, terms_here, terms_far)
    late_in = swap(late_out, 1)
    early_in = swap(early_out, 0)
    tiles = own_update(owners, offsets, object_slices, terms_here, terms_far)
    tiles, whole = early_update(tiles, early_in)
    return late_update(tiles, late_in, whole)


def solution(mesh):
    placed = (
        P(),
        P(),
        P("slab", "scan", None, None),
        P("scan", None, None, None, None),
        P("scan", None, None),
        P("scan", None, None),
    )
    return jax.shard_map(
        shards, mesh=mesh, in_specs=placed, out_specs=P("slab", "scan", None, None), check_vma=False
    )
```

```python
import functools

import jax
import jax.numpy as jnp
from jax import lax
from jax.experimental import pallas as pl
from jax.experimental.pallas import tpu as pltpu
from jax.sharding import PartitionSpec as P

step_rate = 0.125
F32, BF16 = jnp.float32, jnp.bfloat16
NP, TS, HALF = 256, 128, 15
MODES, POS, CAP = 4, 2, 8
STEP = 32
VMEM = pl.BlockSpec(memory_space=pltpu.VMEM)
HBM = pl.BlockSpec(memory_space=pltpu.HBM)


def params(mib):
    return pltpu.CompilerParams(vmem_limit_bytes=mib * 1024 * 1024)


def dot(left, right):
    return jnp.dot(left, right, preferred_element_type=F32)


class Table:
    def __init__(self, values):
        self.values = values.astype(F32)
        self.row, self.lane = (lax.broadcasted_iota(jnp.int32, values.shape, axis) for axis in range(2))

    def at(self, row, lane):
        return jnp.sum(jnp.where((self.row == row) & (self.lane == lane), self.values, 0.0)).astype(jnp.int32)


def lanes(rows):
    return lax.broadcasted_iota(jnp.int32, (rows, TS), 1)


def band(taps, row):
    wide = jnp.broadcast_to(taps[row : row + 1, :], (NP, NP))
    turned = pltpu.roll(wide, NP - HALF, 1, stride=1, stride_axis=0)
    gap = lax.broadcasted_iota(jnp.int32, (NP, NP), 1) - lax.broadcasted_iota(jnp.int32, (NP, NP), 0)
    return jnp.where(jnp.abs(gap) <= HALF, turned, 0.0)


def exit_kernel(taps, residual, left, left_adj, right, right_adj, wave, line):
    line[...] = jnp.zeros_like(line)
    for row in range(4):
        line[row : row + 1, 0 : 2 * HALF + 1] = taps[row // 2, row % 2 : row % 2 + 1, :].astype(F32)
    values = line[...]
    for first, plain, adj in ((0, left, left_adj), (2, right_adj, right)):
        re, im = band(values, first), band(values, first + 1)
        ret, imt = re.T, im.T
        plain[0:NP, 0:NP] = re.astype(BF16)
        plain[0:NP, NP:] = (-im).astype(BF16)
        plain[NP:, 0:NP] = im.astype(BF16)
        plain[NP:, NP:] = re.astype(BF16)
        adj[0:NP, 0:NP] = ret.astype(BF16)
        adj[0:NP, NP:] = imt.astype(BF16)
        adj[NP:, 0:NP] = (-imt).astype(BF16)
        adj[NP:, NP:] = ret.astype(BF16)
    for m in range(MODES):
        w = dot(residual[0, 0, m], right_adj[...]).astype(BF16)
        w = jnp.concatenate([w[:, :NP], w[:, NP:]], 0)
        wave[m] = dot(left_adj[...], w).astype(BF16)


def exit_adjoint(side, taps, residual):
    whole = lambda *shape: pl.BlockSpec(shape, lambda i, side: (0,) * len(shape))
    return pl.pallas_call(
        lambda side, *refs: exit_kernel(*refs),
        grid_spec=pltpu.PrefetchScalarGridSpec(
            num_scalar_prefetch=1,
            grid=(1,),
            in_specs=[
                whole(2, 2, 2 * HALF + 1),
                pl.BlockSpec((1, 1, MODES, NP, 2 * NP), lambda i, side: (0, side[0], 0, 0, 0)),
            ],
            out_specs=[whole(2 * NP, 2 * NP)] * 4 + [whole(MODES, 2 * NP, NP)],
            scratch_shapes=[pltpu.VMEM((8, NP), F32)],
        ),
        out_shape=[jax.ShapeDtypeStruct((2 * NP, 2 * NP), BF16)] * 4
        + [jax.ShapeDtypeStruct((MODES, 2 * NP, NP), BF16)],
        compiler_params=params(24),
        cost_estimate=pl.CostEstimate(flops=1_100_000_000, bytes_accessed=6_000_000, transcendentals=0),
        name="exit_adjoint",
    )(side, taps, residual)


def early_side():
    return 1 - lax.axis_index("scan") % 2


def packed_tile(tiles):
    return lambda q: tiles[q].astype(F32)


def plain_tile(tiles):
    return lambda q: tiles[0, q].astype(BF16).astype(F32)


def cut_column(p, j, owners, offsets, tile_at, stack, put):
    for i in range(3):
        tile = tile_at(owners.at(p, 3 * i + j) & (CAP - 1))
        stack[0, i * TS : (i + 1) * TS, :] = tile[:, :TS]
        stack[1, i * TS : (i + 1) * TS, :] = tile[:, TS:]
    r, c = offsets.at(p, 0), offsets.at(p, 1)
    back = (TS - c) & (TS - 1)
    for at in range(0, NP, STEP):
        for part in range(2):
            put(part, at, pltpu.roll(stack[part, pl.ds(r + at, STEP), :], back, 1))


def half(side):
    return pl.ds(pl.multiple_of(side * TS, TS), TS)


def taken(side, c):
    past = lanes(STEP) - (TS - c)
    return past * (1 - 2 * side) - side < 0


def early_kernel(owners, offsets, own, early, out, stack):
    owners, offsets = Table(owners[0]), Table(offsets[0])
    side = early_side()
    for p in range(POS):

        def put_own(part, at, turned):
            out[p, part, at : at + STEP, :TS] = turned
            out[p, part, at : at + STEP, TS:] = turned

        cut_column(p, 1, owners, offsets, plain_tile(own), stack.at[0], put_own)
        mask = taken(side, offsets.at(p, 1))

        def put_early(part, at, turned):
            place = (p, part, slice(at, at + STEP), half(side))
            out[place] = jnp.where(mask, turned, out[place])

        cut_column(p, 2 * side, owners, offsets, packed_tile(early), stack.at[1], put_early)


def early_windows(owners, offsets, own, early):
    return pl.pallas_call(
        early_kernel,
        out_shape=jax.ShapeDtypeStruct((POS, 2, NP, NP), F32),
        in_specs=[VMEM] * 4,
        out_specs=VMEM,
        scratch_shapes=[pltpu.VMEM((2, 2, 3 * TS, TS), F32)],
        compiler_params=params(8),
        cost_estimate=pl.CostEstimate(flops=2_000_000, bytes_accessed=2_000_000, transcendentals=0),
        name="early_windows",
    )(owners, offsets, own, early)


def complete(p, owners, offsets, late, partly, stack, out):
    side = 1 - early_side()
    mask = taken(side, offsets.at(p, 1))

    def put(part, at, turned):
        rows = slice(at, at + STEP)
        kept = partly[p, part, rows, half(side)]
        out[part, rows, half(side)] = jnp.where(mask, turned, kept).astype(out.dtype)
        out[part, rows, half(1 - side)] = partly[p, part, rows, half(1 - side)].astype(out.dtype)

    cut_column(p, 2 * side, owners, offsets, packed_tile(late), stack, put)


def late_kernel(owners, offsets, late, partly, far, near, stack):
    owners, offsets = Table(owners[0]), Table(offsets[0])
    here = lax.axis_index("slab")
    complete(1 - here, owners, offsets, late, partly, stack.at[0], far)
    complete(here, owners, offsets, late, partly, stack.at[1], near)


def late_windows(owners, offsets, late, partly):
    return pl.pallas_call(
        late_kernel,
        out_shape=[jax.ShapeDtypeStruct((2, NP, NP), BF16)] * 2,
        in_specs=[VMEM] * 4,
        out_specs=[VMEM] * 2,
        scratch_shapes=[pltpu.VMEM((2, 2, 3 * TS, TS), F32)],
        compiler_params=params(8),
        cost_estimate=pl.CostEstimate(flops=1_000_000, bytes_accessed=2_000_000, transcendentals=0),
        name="late_windows",
    )(owners, offsets, late, partly)


def times(a, b, conjugate):
    (ar, ai), (br, bi) = a, b
    if conjugate:
        return ar * br + ai * bi, ar * bi - ai * br
    return ar * br - ai * bi, ar * bi + ai * br


def beside(ref, m):
    return ref[m, :, :NP].astype(F32), ref[m, :, NP:].astype(F32)


def above(ref, m):
    return ref[m, :NP, :].astype(F32), ref[m, NP:, :].astype(F32)


def summed(pairs, total):
    for at in range(0, NP, STEP):
        rows = slice(at, at + STEP)
        re = im = None
        for left, right in pairs(rows):
            one_re, one_im = times(left, right, True)
            re, im = (one_re, one_im) if re is None else (re + one_re, im + one_im)
        total[0, rows, :], total[1, rows, :] = re.astype(total.dtype), im.astype(total.dtype)


def wide(ref, m, rows):
    return ref[m, rows, :NP].astype(F32), ref[m, rows, NP:].astype(F32)


def tall(ref, m, rows):
    return ref[m, rows, :].astype(F32), ref[m, slice(NP + rows.start, NP + rows.stop), :].astype(F32)


def lower_terms(t, probe, wave, left, right, total, rows_in, waves):
    window = (t[0].astype(F32), t[1].astype(F32))
    for m in range(MODES):
        u = jnp.concatenate(times(beside(probe, m), window, False), 0).astype(BF16)
        v = dot(left[...], u).astype(BF16)
        rows_in[m * NP : (m + 1) * NP, :NP] = v[:NP]
        rows_in[m * NP : (m + 1) * NP, NP:] = v[NP:]
    waves[...] = dot(rows_in[...], right[...]).reshape(MODES, NP, 2 * NP)
    summed(lambda rows: [(wide(waves, m, rows), tall(wave, m, rows)) for m in range(MODES)], total)


def upper_terms(t, probe, wave, left_adj, right_adj, total, rows_in, waves):
    window = (t[0].astype(F32), t[1].astype(F32))
    for m in range(MODES):
        re, im = times(window, above(wave, m), True)
        rows_in[m * NP : (m + 1) * NP, :NP] = re.astype(BF16)
        rows_in[m * NP : (m + 1) * NP, NP:] = im.astype(BF16)
    w = dot(rows_in[...], right_adj[...]).astype(BF16)
    for m in range(MODES):
        part = w[m * NP : (m + 1) * NP]
        waves[m] = dot(left_adj[...], jnp.concatenate([part[:, :NP], part[:, NP:]], 0))
    summed(lambda rows: [(wide(probe, m, rows), tall(waves, m, rows)) for m in range(MODES)], total)


def terms_kernel(far, t, probe, wave, left, left_adj, right, right_adj, out, rows_in, lower, upper):
    side = lax.axis_index("slab")
    chosen = 1 - side if far else side

    @pl.when(chosen == 0)
    def _():
        lower_terms(t, probe, wave, left, right, out, rows_in, lower)

    @pl.when(chosen == 1)
    def _():
        upper_terms(t, probe, wave, left_adj, right_adj, out, rows_in, upper)


def slice_terms(far, t, probe, wave, mats):
    return pl.pallas_call(
        functools.partial(terms_kernel, far),
        out_shape=jax.ShapeDtypeStruct((2, NP, NP), F32 if far else BF16),
        in_specs=[VMEM] * 7,
        out_specs=VMEM,
        scratch_shapes=[
            pltpu.VMEM((MODES * NP, 2 * NP), BF16),
            pltpu.VMEM((MODES, NP, 2 * NP), F32),
            pltpu.VMEM((MODES, 2 * NP, NP), F32),
        ],
        compiler_params=params(32),
        cost_estimate=pl.CostEstimate(flops=1_100_000_000, bytes_accessed=5_000_000, transcendentals=0),
        name="far_terms" if far else "near_terms",
    )(t, probe, wave, *mats)


def split_kernel(owners, offsets, mine, others, early, late, notes):
    here = lax.axis_index("slab")
    notes[...] = jnp.zeros_like(notes)
    notes[0:POS, 0:9] = (owners[0] & (CAP - 1)).astype(F32)
    notes[POS : 2 * POS, 0:2] = offsets[0].astype(F32)
    early[POS * NP :, :] = notes[...].astype(BF16)
    late[POS * NP :, :] = notes[...].astype(BF16)
    offsets = Table(offsets[0])
    to_right = early_side() == 1
    spot = lanes(STEP)
    for k, terms in ((0, mine), (1, others)):
        p = here if k == 0 else 1 - here
        c = offsets.at(p, 1)
        for at in range(0, NP, STEP):
            for part in range(2):
                low = pltpu.roll(terms[part, at : at + STEP, 0:TS].astype(F32), c, 1)
                high = pltpu.roll(terms[part, at : at + STEP, TS:].astype(F32), c, 1)
                place = (pl.ds(p * NP + at, STEP), slice(part * TS, (part + 1) * TS))
                left = jnp.where(spot >= c, low, 0.0)
                right = jnp.where(spot < c, high, 0.0)
                early[place] = jnp.where(to_right, right, left).astype(BF16)
                late[place] = jnp.where(to_right, left, right).astype(BF16)


def split_terms(owners, offsets, mine, others):
    sent = jax.ShapeDtypeStruct((POS * NP + 16, 2 * TS), BF16)
    return pl.pallas_call(
        split_kernel,
        out_shape=[sent, sent],
        in_specs=[VMEM] * 4,
        out_specs=[VMEM] * 2,
        scratch_shapes=[pltpu.VMEM((16, 2 * TS), F32)],
        compiler_params=params(8),
        name="split_terms",
    )(owners, offsets, mine, others)


STACK = pltpu.VMEM((POS, 2, 2 * TS + NP, TS), F32)


def clear(stack):
    for p in range(POS):
        for part in range(2):
            stack[p, part, :TS, :] = jnp.zeros((TS, TS), F32)
            stack[p, part, TS + NP :, :] = jnp.zeros((TS, TS), F32)


def fill(terms, stack):
    clear(stack)
    for p in range(POS):
        for part in range(2):
            cols = slice(part * TS, (part + 1) * TS)
            stack[p, part, TS : TS + NP, :] = terms[p * NP : (p + 1) * NP, cols].astype(F32) * step_rate


def starts_of(q, slots, rows):
    starts = []
    for p in range(POS):
        start = jnp.int32(0)
        for i in range(3):
            start = jnp.where(slots[p][i] == q, TS + i * TS - rows[p], start)
        starts.append(start)
    return starts


def subtract(q, pieces, stack, tiles, out):
    for part in range(2):
        cols = slice(part * TS, (part + 1) * TS)
        tile = tiles[0, q, :, cols]
        for p, start in pieces:
            tile = tile - stack[p, part, pl.ds(start, TS), :]
        out[0, q, :, cols] = tile


def take_off(q, slots, rows, stack, tiles, out):
    subtract(q, list(enumerate(starts_of(q, slots, rows))), stack, tiles, out)


def own_kernel(owners, offsets, tiles, mine, others, out, stack):
    owners, offsets = Table(owners[0]), Table(offsets[0])
    here = lax.axis_index("slab")
    spot = lanes(STEP)
    clear(stack)
    for k, terms in ((0, mine), (1, others)):
        p = here if k == 0 else 1 - here
        c = offsets.at(p, 1)
        for at in range(0, NP, STEP):
            for part in range(2):
                low = pltpu.roll(terms[part, at : at + STEP, 0:TS].astype(F32), c, 1)
                high = pltpu.roll(terms[part, at : at + STEP, TS:].astype(F32), c, 1)
                stack[p, part, TS + at : TS + at + STEP, :] = jnp.where(spot < c, low, high) * step_rate
    slots = [[owners.at(p, 3 * i + 1) & (CAP - 1) for i in range(3)] for p in range(POS)]
    for q in range(CAP):
        take_off(q, slots, [offsets.at(p, 0) for p in range(POS)], stack, tiles, out)


def own_update(owners, offsets, tiles, mine, others):
    return pl.pallas_call(
        own_kernel,
        out_shape=jax.ShapeDtypeStruct(tiles.shape, F32),
        in_specs=[VMEM] * 5,
        out_specs=VMEM,
        scratch_shapes=[STACK],
        compiler_params=params(8),
        cost_estimate=pl.CostEstimate(flops=1_000_000, bytes_accessed=3_000_000, transcendentals=0),
        name="own_update",
    )(owners, offsets, tiles, mine, others)


def noted(j, terms):
    notes = Table(terms[POS * NP :, :TS])
    slots = [[notes.at(p, 3 * i + j) for i in range(3)] for p in range(POS)]
    return slots, [notes.at(POS + p, 0) for p in range(POS)]


def early_update_kernel(tiles, terms, out, whole, stack, sems):
    j = 2 - 2 * early_side()
    slots, rows = noted(j, terms)
    fill(terms, stack)
    for q in range(CAP):
        take_off(q, slots, rows, stack, tiles, out)
        pltpu.make_async_copy(out.at[0, q], whole.at[0, q], sems.at[q]).start()
    for q in range(CAP):
        pltpu.make_async_copy(out.at[0, q], whole.at[0, q], sems.at[q]).wait()


def early_update(tiles, terms):
    return pl.pallas_call(
        early_update_kernel,
        out_shape=[jax.ShapeDtypeStruct(tiles.shape, F32)] * 2,
        in_specs=[VMEM, VMEM],
        out_specs=[VMEM, HBM],
        scratch_shapes=[STACK, pltpu.SemaphoreType.DMA((CAP,))],
        compiler_params=params(8),
        cost_estimate=pl.CostEstimate(flops=1_000_000, bytes_accessed=3_000_000, transcendentals=0),
        name="early_update",
    )(tiles, terms)


def late_update_kernel(tiles, terms, whole, out, stack, work, sems):
    j = 2 * early_side()
    slots, rows = noted(j, terms)
    fill(terms, stack)
    starts = [starts_of(q, slots, rows) for q in range(CAP)]
    touched = [first + second > 0 for first, second in starts]
    for q, (first, second) in enumerate(starts):

        @pl.when((first > 0) != (second > 0))
        def _():
            subtract(q, [((second > 0).astype(jnp.int32), first + second)], stack, tiles, work)

        @pl.when((first > 0) & (second > 0))
        def _():
            subtract(q, [(0, first), (1, second)], stack, tiles, work)

        @pl.when(touched[q])
        def _():
            pltpu.make_async_copy(work.at[0, q], out.at[0, q], sems.at[q]).start()

    for q in range(CAP):

        @pl.when(touched[q])
        def _():
            pltpu.make_async_copy(work.at[0, q], out.at[0, q], sems.at[q]).wait()


def late_update(tiles, terms, whole):
    return pl.pallas_call(
        late_update_kernel,
        out_shape=jax.ShapeDtypeStruct(tiles.shape, F32),
        in_specs=[VMEM, VMEM, HBM],
        out_specs=HBM,
        input_output_aliases={2: 0},
        scratch_shapes=[STACK, pltpu.VMEM((1, CAP, TS, 2 * TS), F32), pltpu.SemaphoreType.DMA((CAP,))],
        compiler_params=params(8),
        name="late_update",
    )(tiles, terms, whole)


def swap(value, first):
    count = lax.axis_size("scan")
    pairs = [(i, (i + 1) % count) for i in range(first, count, 2)]
    return lax.ppermute(value, "scan", pairs + [(j, i) for i, j in pairs])


def across(value):
    return lax.ppermute(value, "slab", [(0, 1), (1, 0)])


def shards(probe_modes, tap_weights, object_slices, exit_residual, offsets, owners):
    side = lax.axis_index("slab").astype(jnp.int32).reshape(1)
    own = object_slices[0].astype(BF16)
    late = swap(own, 1)
    early = swap(own, 0)
    *mats, wave = exit_adjoint(side, tap_weights, exit_residual)
    partly = early_windows(owners, offsets, object_slices, early)
    t_there, t_near = late_windows(owners, offsets, late, partly)
    t_here = across(t_there)
    terms_there = slice_terms(False, t_near, probe_modes, wave, mats)
    terms_far = across(terms_there)
    terms_here = slice_terms(True, t_here, probe_modes, wave, mats)
    early_out, late_out = split_terms(owners, offsets, terms_here, terms_far)
    late_in = swap(late_out, 1)
    early_in = swap(early_out, 0)
    tiles = own_update(owners, offsets, object_slices, terms_here, terms_far)
    tiles, whole = early_update(tiles, early_in)
    return late_update(tiles, late_in, whole)


def solution(mesh):
    placed = (
        P(),
        P(),
        P("slab", "scan", None, None),
        P("scan", None, None, None, None),
        P("scan", None, None),
        P("scan", None, None),
    )
    return jax.shard_map(
        shards, mesh=mesh, in_specs=placed, out_specs=P("slab", "scan", None, None), check_vma=False
    )
```
